32 devices in a mesh: chrom: 16 (over z, y, x), chan: 2 (over core).
Axes of the slice: x: 2, y: 2, z: 4, core: 2. Of those that a mesh axis runs over, the one named last changes fastest.
Arguments:
- left_embed: bfloat16 [256, 256], P('chrom', 'chan'), may hold values from -6 to 6
- right_embed: bfloat16 [256, 256], P('chrom', 'chan'), may hold values from -6 to 6
- conv_weight: bfloat16 [3, 3, 3, 256, 256], P(None, None, None, None, 'chan'), may hold values from -0.125 to 0.125
- readout: float32 [256], P('chan'), may hold values from -0.375 to 0.375
- cotangent: float32 [256, 64], P('chrom'), may hold values from -6 to 6
Outputs:
- contact: float32 [256, 64], P('chrom')
- left_grad: float32 [256, 256], P('chrom', 'chan')
- right_grad: float32 [256, 256], P('chrom', 'chan')
The draws below stay inside these ranges and needn't reach their ends.
All inputs are finite; a program needn't handle non-finite values.
Results may differ from the reference program's by a relative error of at most 0.013.
Values may be sent and summed in bfloat16 or wider, within the bound.
A program may use at most 64 MiB of HBM per device.

```python
import jax
import jax.numpy as jnp
from jax import lax

C = 256
WIN = 64
LAYERS = 3
L = 256
N_CHAN = 2


def block_levels(key, shape, pieces, low, top_value):
    loudness = 1.0
    for position, shards_of in pieces:
        steps = jax.random.uniform(jax.random.fold_in(jax.random.fold_in(key, 6), position), (shards_of,), jnp.float32, low / len(pieces), top_value / len(pieces))
        loudness = loudness * jnp.repeat(jnp.exp(steps), shape[position] // shards_of).reshape((-1,) + (1,) * (len(shape) - 1 - position))
    return loudness


def noise(rng, shape, width, most, cuts=(), held_as=jnp.bfloat16):
    values = width * jax.random.normal(rng, shape, jnp.float32)
    if cuts:
        values = values * block_levels(rng, shape, cuts, -0.22, 0.18)
    return jnp.clip(values, -most, most).astype(held_as)


def setup_inputs(seed: int = 0) -> dict:
    splits = jax.random.split(jax.random.key(seed), 6)
    left_embed = noise(splits[0], (L, C), 1.0, 6.0, ((0, 16), (1, 2)))
    right_embed = noise(splits[1], (L, C), 1.0, 6.0, ((0, 16), (1, 2)))
    conv_weight = noise(splits[2], (LAYERS, 3, 3, C, C), (9 * C) ** -0.5, 0.125, ((4, 2),))
    readout = noise(splits[3], (C,), C ** -0.5, 0.375, ((0, 2),), jnp.float32)
    cotangent = noise(splits[4], (L, WIN), 1.0, 6.0, ((0, 16),), jnp.float32)
    return dict(left_embed=left_embed, right_embed=right_embed, conv_weight=conv_weight, readout=readout, cotangent=cotangent)


def silu_grad(z):
    s = jax.nn.sigmoid(z)
    return s * (1.0 + z * (1.0 - s))

def reference(left_embed, right_embed, conv_weight, readout, cotangent):
    total_bins = left_embed.shape[0]
    channels = left_embed.shape[1]
    share = channels // N_CHAN
    padded_right = jnp.concatenate([right_embed, jnp.zeros((WIN, channels), jnp.bfloat16)], axis=0)
    index = (jnp.arange(total_bins, dtype=jnp.int32)[:, None] + jnp.arange(WIN, dtype=jnp.int32)[None, :]).astype(jnp.int32)
    pair = (left_embed.astype(jnp.float32)[:, None, :] + padded_right[index].astype(jnp.float32)).astype(jnp.bfloat16)
    states = []
    for layer in range(LAYERS):
        r = 2 ** layer
        padded = jnp.pad(pair, ((r, r), (r, r), (0, 0)))
        pre = jnp.zeros((total_bins, WIN, channels), jnp.float32)
        for a in range(3):
            for b in range(3):
                piece = padded[a * r:a * r + total_bins, b * r:b * r + WIN, :].reshape(-1, channels)
                pre = pre + jnp.dot(piece, conv_weight[layer, a, b], preferred_element_type=jnp.float32).reshape(total_bins, WIN, channels)
        states.append(pre)
        pair = (pair.astype(jnp.float32) + jax.nn.silu(pre)).astype(jnp.bfloat16)
    contact = lax.optimization_barrier(jnp.sum(pair.astype(jnp.float32) * readout[None, None, :], axis=-1))
    grad = cotangent[:, :, None] * readout[None, None, :]
    for layer in reversed(range(LAYERS)):
        r = 2 ** layer
        dpre = (grad * silu_grad(states[layer])).astype(jnp.bfloat16)
        padded = jnp.pad(dpre, ((r, r), (r, r), (0, 0)))
        total = grad
        for group in range(N_CHAN):
            part = jnp.zeros((total_bins, WIN, channels), jnp.float32)
            for a in range(3):
                for b in range(3):
                    piece = padded[(2 - a) * r:(2 - a) * r + total_bins, (2 - b) * r:(2 - b) * r + WIN, group * share:(group + 1) * share].reshape(-1, share)
                    kernel = conv_weight[layer, a, b][:, group * share:(group + 1) * share]
                    part = part + jnp.dot(piece, kernel.T, preferred_element_type=jnp.float32).reshape(total_bins, WIN, channels)
            total = total + part.astype(jnp.bfloat16).astype(jnp.float32)
        grad = total
    left_grad = lax.optimization_barrier(jnp.sum(grad, axis=1))

    def add_diagonal(step, acc):
        column = lax.dynamic_index_in_dim(grad, step, 1, keepdims=False)
        start = step.astype(jnp.int32)
        current = lax.dynamic_slice_in_dim(acc, start, total_bins, 0)
        return lax.dynamic_update_slice_in_dim(acc, current + column, start, 0)
    accum = lax.fori_loop(0, WIN, add_diagonal, jnp.zeros((total_bins + WIN, channels), jnp.float32))
    right_grad = accum[:total_bins]
    return (contact, left_grad, right_grad)
```

```python
import functools

import jax
import jax.numpy as jnp
from jax import lax
from jax.experimental import pallas as pl
from jax.experimental.pallas import tpu as pltpu
from jax.sharding import PartitionSpec as P

MESH = pl.DeviceIdType.MESH
F32, BF16 = jnp.float32, jnp.bfloat16
BACK, AHEAD = 1, 5
Q = 4


def split3(x):
    hi = x.astype(BF16)
    rest = x - hi.astype(F32)
    mid = rest.astype(BF16)
    return hi, mid, (rest - mid.astype(F32)).astype(BF16)


def nt(a, b):
    return lax.dot_general(a, b, (((1,), (1,)), ((), ())), preferred_element_type=F32)


def shifted(x, step):
    n = x.shape[2]
    flat = x.reshape((x.shape[0] * x.shape[1],) + x.shape[2:])
    moved = pltpu.roll(flat, step % n, 1)
    where = lax.broadcasted_iota(jnp.int32, flat.shape, 1)
    edge = 0 if step == 1 else n - 1
    return jnp.where(where == edge, 0.0, moved).reshape(x.shape)


def put(buf, row, x, r):
    rows = pl.ds(row, x.shape[0])
    buf[rows, r : r + Q] = x.astype(BF16)
    buf[rows, 0:r] = shifted(x[:, Q - r :], 1).astype(BF16)
    buf[rows, r + Q :] = shifted(x[:, :r], -1).astype(BF16)


def kernel(
    slabs,
    left_ref, right_ref, w_hbm, ro_ref, cot_ref,
    contact_out, lg_out, rg_out,
    block, emb, rwin, w, cot, ro, p0, p1, p2, d2, d1, d0, s0, s1, g2, g1,
    spread, rg, swap_out, swap,
    emb_ss, emb_rs, w_ls, w_ss, w_rs, cot_ss, cot_rs, ro_ss, ro_rs, rg_ss, rg_rs, swap_ss, swap_rs,
):
    slab = lax.axis_index("chrom")
    half = lax.axis_index("chan")
    mate = 1 - half

    def there(delta):
        return jnp.logical_and(slab + delta >= 0, slab + delta < slabs)

    def send(src, dst, ss, rs, delta, chan):
        return pltpu.make_async_remote_copy(
            src_ref=src, dst_ref=dst, send_sem=ss, recv_sem=rs,
            device_id=(slab + delta, chan), device_id_type=MESH,
        )

    barrier = pltpu.get_barrier_semaphore()
    reach = max(BACK, AHEAD)
    for delta in range(-reach, reach + 1):
        if delta == 0:
            pl.semaphore_signal(barrier, inc=1, device_id=(slab, mate), device_id_type=MESH)
        else:
            @pl.when(there(delta))
            def _(delta=delta):
                for chan in range(2):
                    pl.semaphore_signal(barrier, inc=1, device_id=(slab + delta, chan), device_id_type=MESH)

    layers = w.shape[1]
    local = [pltpu.make_async_copy(w_hbm.at[k], w.at[half, k], w_ls.at[k]) for k in range(layers)]
    for copy in local:
        copy.start()
    block[0:16] = right_ref[...]
    block[16:32] = left_ref[...]
    emb[BACK, half] = block[...]
    cot[16:32] = jnp.concatenate([cot_ref[...], jnp.zeros((16, 64), F32)], axis=1)
    ro[half] = jnp.broadcast_to(ro_ref[...], (8, 128))
    for k in range(BACK + AHEAD + 1):
        if k != BACK:
            @pl.when(jnp.logical_not(there(k - BACK)))
            def _(k=k):
                emb[k] = jnp.zeros(emb.shape[1:], BF16)
    for delta in (-1, 1):
        @pl.when(jnp.logical_not(there(delta)))
        def _(delta=delta):
            cot[16 + 16 * delta : 32 + 16 * delta] = jnp.zeros((16, 128), F32)

    pl.semaphore_wait(
        barrier, 2 * (jnp.minimum(slab, reach) + jnp.minimum(slabs - 1 - slab, reach) + 1) - 1
    )

    def emb_copy(delta, chan):
        k = BACK - delta
        return send(block, emb.at[k, half], emb_ss.at[k, chan], emb_rs.at[k, half], delta, chan)

    def each_emb(act):
        for delta in (0, 1, -1, -2, -3, -4, -5):
            if delta == 0:
                act(emb_copy(0, mate))
            else:
                @pl.when(there(delta))
                def _(delta=delta):
                    for chan in range(2):
                        act(emb_copy(delta, chan))

    def w_copy(k):
        return send(w_hbm.at[k], w.at[half, k], w_ss.at[k], w_rs.at[k], 0, mate)

    def cot_copy(delta):
        place = pl.ds(16 - 16 * delta, 16)
        slot = (1 - delta) // 2
        return send(cot.at[pl.ds(16, 16)], cot.at[place], cot_ss.at[slot], cot_rs.at[slot], delta, half)

    def each_cot(act):
        for delta in (-1, 1):
            @pl.when(there(delta))
            def _(delta=delta):
                act(cot_copy(delta))

    ro_copy = send(ro.at[half], ro.at[half], ro_ss.at[0], ro_rs.at[0], 0, mate)

    each_emb(lambda c: c.start())
    for k in range(layers):
        w_copy(k).start()
    ro_copy.start()
    each_cot(lambda c: c.start())

    def emb_wait(k, chan):
        send(block, emb.at[k, chan], emb_ss.at[k, chan], emb_rs.at[k, chan], 0, mate).wait_recv()

    for k in range(BACK + AHEAD + 1):
        if k == BACK:
            emb_wait(k, mate)
        else:
            @pl.when(there(k - BACK))
            def _(k=k):
                for chan in range(2):
                    emb_wait(k, chan)

    for k in range(BACK + AHEAD + 1):
        for c in range(2):
            rwin[c, 16 * k : 16 * k + 16] = emb[k, c, 0:16].astype(F32)
            if k < 3:
                rwin[2 + c, 16 * k : 16 * k + 16] = emb[k, c, 16:32].astype(F32)
    start = pl.multiple_of(8 * half, 8)
    for c in range(2):
        rwin[c, 0:104] = rwin[c, pl.ds(start, 104)]
    lwin = jnp.concatenate([rwin[2 + c, pl.ds(start, 40)] for c in range(2)], axis=1)

    def clear(buf, first, count):
        for h in range(2):
            low, high = 16 - 8 * h, 32 - 8 * h
            if first < low:
                @pl.when(jnp.logical_and(slab == 0, half == h))
                def _():
                    n = min(low, first + count) - first
                    buf[0:n] = jnp.zeros((n,) + buf.shape[1:], BF16)
            if first + count > high:
                @pl.when(jnp.logical_and(slab == slabs - 1, half == h))
                def _():
                    begin = max(high - first, 0)
                    buf[begin:count] = jnp.zeros((count - begin,) + buf.shape[1:], BF16)

    diag = {}
    for i in range(36):
        tiles = []
        for q in range(Q):
            t = 2 + i + q
            if t not in diag:
                diag[t] = jnp.concatenate([rwin[c, pl.ds(t, 16, stride=Q), :] for c in range(2)], axis=1)
            tiles.append(diag[t] + lwin[2 + i : 3 + i, :])
        put(p0, i, jnp.stack(tiles)[None], 1)
    clear(p0, 2, 36)

    def weights(k):
        local[k].wait()
        send(w_hbm.at[k], w.at[mate, k], w_ss.at[k], w_rs.at[k], 0, mate).wait_recv()

    def forward(k, src, src_first, first, count, chunk, sink):
        r = 2**k
        weights(k)
        wide = jnp.concatenate([w[c, k].reshape(9 * 256, 128) for c in range(2)], axis=1)
        for begin in range(first, first + count, chunk):
            n = min(chunk, first + count - begin)
            lhs = jnp.concatenate(
                [
                    src[pl.ds(begin + (a - 1) * r - src_first, n), b * r : b * r + Q].reshape(n * 64, 256)
                    for a in range(3) for b in range(3)
                ],
                axis=1,
            )
            z = jnp.dot(lhs, wide, preferred_element_type=F32).reshape(n, Q, 16, 256)
            s = 0.5 + 0.5 * jnp.tanh(0.5 * z)
            old = src[pl.ds(begin - src_first, n), r : r + Q].astype(F32)
            zs = z * s
            sink(begin, n, old + zs, s + zs * (1.0 - s))

    def keep(buf, buf_first, r, slopes, slopes_first):
        count = slopes.shape[0]

        def sink(begin, n, x, slope):
            if buf is not None:
                put(buf, begin - buf_first, x, r)
            low, high = max(begin, slopes_first), min(begin + n, slopes_first + count)
            if low < high:
                slopes[pl.ds(low - slopes_first, high - low)] = slope[low - begin : high - begin]

        return sink

    forward(0, p0, 2, 3, 34, 9, keep(p1, 3, 2, s0, 15))
    clear(p1, 3, 34)
    forward(1, p1, 3, 5, 30, 10, keep(p2, 5, 4, s1, 13))
    clear(p2, 5, 30)

    n_i = lax.broadcasted_iota(jnp.int32, (64, 128), 0)
    d_i = lax.broadcasted_iota(jnp.int32, (64, 128), 1)
    order = jnp.where(d_i == Q * (n_i % 16) + n_i // 16, 1.0, 0.0).astype(BF16)

    send(ro.at[half], ro.at[mate], ro_ss.at[0], ro_rs.at[0], 0, mate).wait_recv()
    for delta in (-1, 1):
        @pl.when(there(delta))
        def _(delta=delta):
            slot = (1 + delta) // 2
            send(
                cot.at[pl.ds(16, 16)], cot.at[pl.ds(16 + 16 * delta, 16)],
                cot_ss.at[slot], cot_rs.at[slot], delta, half,
            ).wait_recv()
    readout = jnp.concatenate([ro[0, 0:1], ro[1, 0:1]], axis=1)
    parts = split3(readout)
    row_i = lax.broadcasted_iota(jnp.int32, (16, 256), 0)
    ro_rows = sum(
        jnp.where(row_i == m, jnp.broadcast_to(part.astype(F32), (16, 256)), 0.0) for m, part in enumerate(parts)
    ).astype(BF16)
    cot_win = cot[pl.ds(pl.multiple_of(8 * half + 8, 8), 24), :]
    cot_t = sum(nt(order, part) for part in split3(cot_win))

    def top(begin, n):
        return jnp.stack(
            [(cot_t[:, i - 8 : i - 7] * readout).reshape(Q, 16, 256) for i in range(begin, begin + n)]
        )

    contacts = {}

    def last_sink(begin, n, x, slope):
        for i in range(max(begin, 16), min(begin + n, 24)):
            flat = x[i - begin].astype(BF16).reshape(64, 256)
            contacts[i] = jnp.sum(nt(ro_rows, flat), axis=0, keepdims=True)
        grad = top(begin, n)
        put(d2, begin - 9, grad * slope, 4)
        low, high = max(begin, 13), min(begin + n, 27)
        if low < high:
            g2[pl.ds(low - 13, high - low)] = grad[low - begin : high - begin]

    forward(2, p2, 5, 9, 22, 11, last_sink)
    clear(d2, 9, 22)
    contact_rows = jnp.concatenate([contacts[i] for i in range(16, 24)], axis=0)
    contact = sum(jnp.dot(part, order, preferred_element_type=F32) for part in split3(contact_rows))

    def backward(k, src, src_first, first, count, before):
        r = 2**k
        lhs = jnp.concatenate(
            [
                src[pl.ds(first - (a - 1) * r - src_first, count), (2 - b) * r : (2 - b) * r + Q].reshape(count * 64, 256)
                for a in range(3) for b in range(3)
            ],
            axis=1,
        )
        wide = jnp.concatenate([w[c, k, a, b] for a in range(3) for b in range(3) for c in range(2)], axis=1)
        return before + nt(lhs, wide).reshape(count, Q, 16, 256)

    grad = backward(2, d2, 9, 13, 14, g2[...])
    put(d1, 0, grad * s1[...], 2)
    clear(d1, 13, 14)
    g1[...] = grad[2:12]
    grad = backward(1, d1, 13, 15, 10, g1[...])
    put(d0, 0, grad * s0[...], 1)
    clear(d0, 15, 10)
    grad = backward(0, d0, 15, 16, 8, grad[1:9])

    spread[...] = jnp.zeros(spread.shape, F32)
    for t in range(8 + Q - 1):
        total = sum(grad[t - q, q] for q in range(Q) if 0 <= t - q < 8)
        place = pl.ds(8 + t, 16, stride=Q)
        for c in range(2):
            spread[c, place, :] = spread[c, place, :] + total[:, 128 * c : 128 * c + 128]

    def rg_source(k, chan):
        return spread.at[chan, pl.ds(pl.multiple_of(8 - 8 * half + 16 * k, 8), 16)]

    def rg_copy(k, chan):
        return send(rg_source(k, chan), rg.at[k, half], rg_ss.at[k, chan], rg_rs.at[k, half], k, chan)

    def each_rg(act):
        for k in (4, 3, 2, 1, 0):
            if k == 0:
                act(rg_copy(0, mate))
            else:
                @pl.when(there(k))
                def _(k=k):
                    for chan in range(2):
                        act(rg_copy(k, chan))

    each_rg(lambda c: c.start())
    lg = jnp.sum(grad.reshape(8, 64, 256), axis=1)
    low, high = lg[:, :128], lg[:, 128:]
    swap_out[0:8] = jnp.where(half == 0, high, low)
    swap_out[8:16] = contact
    swap_copy = send(swap_out, swap, swap_ss.at[0], swap_rs.at[0], 0, mate)
    swap_copy.start()
    rg[0, half] = spread[half, pl.ds(pl.multiple_of(8 - 8 * half, 8), 16), :]
    mine = pl.ds(pl.multiple_of(8 * half, 8), 8)
    other = pl.ds(pl.multiple_of(8 * mate, 8), 8)
    lg_out[mine, :] = jnp.where(half == 0, low, high)
    contact_out[mine, :] = contact[:, :64]

    for k in range(1, 5):
        @pl.when(jnp.logical_not(there(-k)))
        def _(k=k):
            rg[k] = jnp.zeros(rg.shape[1:], F32)

    swap_copy.wait_recv()
    lg_out[other, :] = swap[0:8]
    contact_out[other, :] = swap[8:16, :64]

    def rg_wait(k, chan):
        send(rg_source(k, chan), rg.at[k, chan], rg_ss.at[k, chan], rg_rs.at[k, chan], 0, mate).wait_recv()

    for k in range(5):
        if k == 0:
            rg_wait(0, mate)
        else:
            @pl.when(there(-k))
            def _(k=k):
                for chan in range(2):
                    rg_wait(k, chan)
    rg_out[...] = sum(rg[k, c] for k in range(5) for c in range(2))

    each_emb(lambda c: c.wait_send())
    for k in range(layers):
        w_copy(k).wait_send()
    ro_copy.wait_send()
    each_cot(lambda c: c.wait_send())
    each_rg(lambda c: c.wait_send())
    swap_copy.wait_send()


def local(slabs, left_embed, right_embed, conv_weight, readout, cotangent):
    vmem = pl.BlockSpec(memory_space=pltpu.VMEM)
    dma = pltpu.SemaphoreType.DMA

    def padded(rows, r):
        return pltpu.VMEM((rows, Q + 2 * r, 16, 256), BF16)

    def wide(rows):
        return pltpu.VMEM((rows, Q, 16, 256), F32)

    return pl.pallas_call(
        functools.partial(kernel, slabs),
        out_shape=(
            jax.ShapeDtypeStruct((16, 64), F32),
            jax.ShapeDtypeStruct((16, 128), F32),
            jax.ShapeDtypeStruct((16, 128), F32),
        ),
        in_specs=[vmem, vmem, pl.BlockSpec(memory_space=pl.ANY), vmem, vmem],
        out_specs=(vmem, vmem, vmem),
        scratch_shapes=[
            pltpu.VMEM((32, 128), BF16),
            pltpu.VMEM((7, 2, 32, 128), BF16),
            pltpu.VMEM((4, 112, 128), F32),
            pltpu.VMEM((2, 3, 3, 3, 256, 128), BF16),
            pltpu.VMEM((48, 128), F32),
            pltpu.VMEM((2, 8, 128), F32),
            padded(36, 1), padded(34, 2), padded(30, 4),
            padded(22, 4), padded(14, 2), padded(10, 1),
            wide(10), wide(14), wide(14), wide(10),
            pltpu.VMEM((2, 88, 128), F32),
            pltpu.VMEM((5, 2, 16, 128), F32),
            pltpu.VMEM((16, 128), F32),
            pltpu.VMEM((16, 128), F32),
            dma((7, 2)), dma((7, 2)), dma((3,)), dma((3,)), dma((3,)),
            dma((2,)), dma((2,)), dma((1,)), dma((1,)),
            dma((5, 2)), dma((5, 2)), dma((1,)), dma((1,)),
        ],
        compiler_params=pltpu.CompilerParams(
            collective_id=0, has_side_effects=True, vmem_limit_bytes=56 * 2**20
        ),
        cost_estimate=pl.CostEstimate(flops=8 * 10**9, bytes_accessed=4 * 10**6, transcendentals=10**6),
    )(left_embed, right_embed, conv_weight, readout.reshape(1, 128), cotangent)


def solution(mesh):
    return jax.shard_map(
        functools.partial(local, mesh.shape["chrom"]),
        mesh=mesh,
        in_specs=(
            P("chrom", "chan"),
            P("chrom", "chan"),
            P(None, None, None, None, "chan"),
            P("chan"),
            P("chrom", None),
        ),
        out_specs=(P("chrom", None), P("chrom", "chan"), P("chrom", "chan")),
        check_vma=False,
    )
```

```python
import functools

import jax
import jax.numpy as jnp
from jax import lax
from jax.experimental import pallas as pl
from jax.experimental.pallas import tpu as pltpu
from jax.sharding import PartitionSpec as P

MESH = pl.DeviceIdType.MESH
F32, BF16 = jnp.float32, jnp.bfloat16
BACK, AHEAD = 1, 5
Q = 4


def split3(x):
    hi = x.astype(BF16)
    rest = x - hi.astype(F32)
    mid = rest.astype(BF16)
    return hi, mid, (rest - mid.astype(F32)).astype(BF16)


def nt(a, b):
    return lax.dot_general(a, b, (((1,), (1,)), ((), ())), preferred_element_type=F32)


def shifted(x, step):
    n = x.shape[2]
    flat = x.reshape((x.shape[0] * x.shape[1],) + x.shape[2:])
    moved = pltpu.roll(flat, step % n, 1)
    where = lax.broadcasted_iota(jnp.int32, flat.shape, 1)
    edge = 0 if step == 1 else n - 1
    return jnp.where(where == edge, 0.0, moved).reshape(x.shape)


def put(buf, row, x, r):
    rows = pl.ds(row, x.shape[0])
    buf[rows, r : r + Q] = x.astype(BF16)
    buf[rows, 0:r] = shifted(x[:, Q - r :], 1).astype(BF16)
    buf[rows, r + Q :] = shifted(x[:, :r], -1).astype(BF16)


def kernel(
    slabs,
    left_ref, right_ref, w_hbm, ro_ref, cot_ref,
    contact_out, lg_out, rg_out,
    block, emb, rwin, w, cot, ro, p0, p1, p2, d2, d1, d0, s0, s1, g2, g1, g0,
    spread, rg, swap_out, swap,
    emb_ss, emb_rs, w_ls, w_ss, w_rs, cot_ss, cot_rs, ro_ss, ro_rs, rg_ss, rg_rs, swap_ss, swap_rs, rim_ss, rim_rs,
):
    slab = lax.axis_index("chrom")
    half = lax.axis_index("chan")
    mate = 1 - half

    def there(delta):
        return jnp.logical_and(slab + delta >= 0, slab + delta < slabs)

    def send(src, dst, ss, rs, delta, chan):
        return pltpu.make_async_remote_copy(
            src_ref=src, dst_ref=dst, send_sem=ss, recv_sem=rs,
            device_id=(slab + delta, chan), device_id_type=MESH,
        )

    barrier = pltpu.get_barrier_semaphore()
    reach = max(BACK, AHEAD)
    for delta in range(-reach, reach + 1):
        if delta == 0:
            pl.semaphore_signal(barrier, inc=1, device_id=(slab, mate), device_id_type=MESH)
        else:
            @pl.when(there(delta))
            def _(delta=delta):
                for chan in range(2):
                    pl.semaphore_signal(barrier, inc=1, device_id=(slab + delta, chan), device_id_type=MESH)

    layers = w.shape[1]
    local = [pltpu.make_async_copy(w_hbm.at[k], w.at[half, k], w_ls.at[k]) for k in range(layers)]
    for copy in local:
        copy.start()
    block[0:16] = right_ref[...]
    block[16:32] = left_ref[...]
    emb[BACK, half] = block[...]
    cot[16:32] = jnp.concatenate([cot_ref[...], jnp.zeros((16, 64), F32)], axis=1)
    ro[half] = jnp.broadcast_to(ro_ref[...], (8, 128))
    for k in range(BACK + AHEAD + 1):
        if k != BACK:
            @pl.when(jnp.logical_not(there(k - BACK)))
            def _(k=k):
                emb[k] = jnp.zeros(emb.shape[1:], BF16)
    for delta in (-1, 1):
        @pl.when(jnp.logical_not(there(delta)))
        def _(delta=delta):
            cot[16 + 16 * delta : 32 + 16 * delta] = jnp.zeros((16, 128), F32)

    pl.semaphore_wait(
        barrier, 2 * (jnp.minimum(slab, reach) + jnp.minimum(slabs - 1 - slab, reach) + 1) - 1
    )

    def emb_copy(delta, chan):
        k = BACK - delta
        return send(block, emb.at[k, half], emb_ss.at[k, chan], emb_rs.at[k, half], delta, chan)

    def each_emb(act):
        for delta in (0, 1, -1, -2, -3, -4, -5):
            if delta == 0:
                act(emb_copy(0, mate))
            else:
                @pl.when(there(delta))
                def _(delta=delta):
                    for chan in range(2):
                        act(emb_copy(delta, chan))

    def w_copy(k):
        return send(w_hbm.at[k], w.at[half, k], w_ss.at[k], w_rs.at[k], 0, mate)

    def cot_copy(delta):
        place = pl.ds(16 - 16 * delta, 16)
        slot = (1 - delta) // 2
        return send(cot.at[pl.ds(16, 16)], cot.at[place], cot_ss.at[slot], cot_rs.at[slot], delta, half)

    def each_cot(act):
        for delta in (-1, 1):
            @pl.when(there(delta))
            def _(delta=delta):
                act(cot_copy(delta))

    ro_copy = send(ro.at[half], ro.at[half], ro_ss.at[0], ro_rs.at[0], 0, mate)

    each_emb(lambda c: c.start())
    for k in range(layers):
        w_copy(k).start()
    ro_copy.start()
    each_cot(lambda c: c.start())

    def emb_wait(k, chan):
        send(block, emb.at[k, chan], emb_ss.at[k, chan], emb_rs.at[k, chan], 0, mate).wait_recv()

    for k in range(BACK + AHEAD + 1):
        if k == BACK:
            emb_wait(k, mate)
        else:
            @pl.when(there(k - BACK))
            def _(k=k):
                for chan in range(2):
                    emb_wait(k, chan)

    for k in range(BACK + AHEAD + 1):
        for c in range(2):
            rwin[c, 16 * k : 16 * k + 16] = emb[k, c, 0:16].astype(F32)
            if k < 3:
                rwin[2 + c, 16 * k : 16 * k + 16] = emb[k, c, 16:32].astype(F32)

    sign = 2 * half - 1

    def bin_of(v):
        return 7 + half + sign * v

    outer_edge = jnp.logical_or(
        jnp.logical_and(half == 0, slab == 0), jnp.logical_and(half == 1, slab == slabs - 1)
    )

    def clear(buf, r):
        @pl.when(outer_edge)
        def _():
            buf[r + 8 :] = jnp.zeros((buf.shape[0] - r - 8,) + buf.shape[1:], BF16)

    def rim(n, buf, r):
        return [
            send(buf.at[r + j], buf.at[r - 1 - j], rim_ss.at[n, j], rim_rs.at[n, j], 0, mate)
            for j in range(r)
        ]

    rims = [rim(n, buf, r) for n, (buf, r) in enumerate([(p1, 2), (p2, 4), (d2, 4), (d1, 2), (d0, 1)])]

    def rim_start(n):
        for copy in rims[n]:
            copy.start()

    def rim_wait(n):
        for copy in rims[n]:
            copy.wait_recv()

    for v in range(-1, 22):
        place = 16 + bin_of(v)
        left = jnp.concatenate([rwin[2 + c, pl.ds(place, 1), :] for c in range(2)], axis=1)
        tiles = [
            left + jnp.concatenate([rwin[c, pl.ds(place + q, 16, stride=Q), :] for c in range(2)], axis=1)
            for q in range(Q)
        ]
        put(p0, v + 1, jnp.stack(tiles)[None], 1)
    clear(p0, 1)

    taps = [2 - 2 * half, 1, 2 * half]

    def weights(k):
        local[k].wait()
        send(w_hbm.at[k], w.at[mate, k], w_ss.at[k], w_rs.at[k], 0, mate).wait_recv()

    def forward(k, src, chunks, sink):
        r = 2**k
        weights(k)
        wide = jnp.concatenate(
            [jnp.concatenate([w[c, k, a].reshape(3 * 256, 128) for a in taps], axis=0) for c in range(2)], axis=1
        )
        begin = 0
        for n in chunks:
            lhs = jnp.concatenate(
                [
                    src[pl.ds(begin + m * r, n), b * r : b * r + Q].reshape(n * 64, 256)
                    for m in range(3) for b in range(3)
                ],
                axis=1,
            )
            z = jnp.dot(lhs, wide, preferred_element_type=F32).reshape(n, Q, 16, 256)
            s = 0.5 + 0.5 * jnp.tanh(0.5 * z)
            old = src[pl.ds(begin + r, n), r : r + Q].astype(F32)
            zs = z * s
            sink(begin, n, old + zs, s + zs * (1.0 - s))
            begin += n

    def keep(buf, r, slopes, n_rim):
        def sink(begin, n, x, slope):
            put(buf, begin + r, x, r)
            if begin == 0:
                rim_start(n_rim)
            kept = min(begin + n, slopes.shape[0]) - begin
            if kept > 0:
                slopes[pl.ds(begin, kept)] = slope[:kept]

        return sink

    forward(0, p0, (11, 10), keep(p1, 2, s0, 0))
    clear(p1, 2)
    rim_wait(0)
    forward(1, p1, (10, 9), keep(p2, 4, s1, 1))
    clear(p2, 4)

    n_i = lax.broadcasted_iota(jnp.int32, (64, 128), 0)
    d_i = lax.broadcasted_iota(jnp.int32, (64, 128), 1)
    order = jnp.where(d_i == Q * (n_i % 16) + n_i // 16, 1.0, 0.0).astype(BF16)

    send(ro.at[half], ro.at[mate], ro_ss.at[0], ro_rs.at[0], 0, mate).wait_recv()
    for delta in (-1, 1):
        @pl.when(there(delta))
        def _(delta=delta):
            slot = (1 + delta) // 2
            send(
                cot.at[pl.ds(16, 16)], cot.at[pl.ds(16 + 16 * delta, 16)],
                cot_ss.at[slot], cot_rs.at[slot], delta, half,
            ).wait_recv()
    readout = jnp.concatenate([ro[0, 0:1], ro[1, 0:1]], axis=1)
    parts = split3(readout)
    row_i = lax.broadcasted_iota(jnp.int32, (16, 256), 0)
    ro_rows = sum(
        jnp.where(row_i == m, jnp.broadcast_to(part.astype(F32), (16, 256)), 0.0) for m, part in enumerate(parts)
    ).astype(BF16)
    cot_win = jnp.concatenate([cot[pl.ds(16 + bin_of(v), 1), :] for v in range(16)], axis=0)
    cot_t = sum(nt(order, part) for part in split3(cot_win))

    contacts = {}

    def last_sink(begin, n, x, slope):
        grad = jnp.stack(
            [(cot_t[:, v : v + 1] * readout).reshape(Q, 16, 256) for v in range(begin, begin + n)]
        )
        put(d2, begin + 4, grad * slope, 4)
        if begin == 0:
            rim_start(2)
        kept = min(begin + n, 11) - begin
        if kept > 0:
            g2[pl.ds(begin, kept)] = grad[:kept]
        for v in range(begin, min(begin + n, 8)):
            flat = x[v - begin].astype(BF16).reshape(64, 256)
            contacts[v] = jnp.sum(nt(ro_rows, flat), axis=0, keepdims=True)

    rim_wait(1)
    forward(2, p2, (8, 7), last_sink)
    clear(d2, 4)
    outwards = jnp.concatenate([contacts[v] for v in range(8)], axis=0)
    inwards = jnp.concatenate([contacts[7 - v] for v in range(8)], axis=0)
    contact_rows = jnp.where(half == 1, outwards, inwards)
    contact = sum(jnp.dot(part, order, preferred_element_type=F32) for part in split3(contact_rows))

    def backward(k, src, chunks, before, sink):
        r = 2**k
        wide = jnp.concatenate([w[c, k, a, b] for a in taps for b in range(3) for c in range(2)], axis=1)
        begin = 0
        for n in chunks:
            lhs = jnp.concatenate(
                [
                    src[pl.ds(begin + (2 - m) * r, n), (2 - b) * r : (2 - b) * r + Q].reshape(n * 64, 256)
                    for m in range(3) for b in range(3)
                ],
                axis=1,
            )
            sink(begin, n, before[pl.ds(begin, n)] + nt(lhs, wide).reshape(n, Q, 16, 256))
            begin += n

    def hand_on(buf, r, slopes, grads, n_rim):
        def sink(begin, n, grad):
            put(buf, begin + r, grad * slopes[pl.ds(begin, n)], r)
            if begin == 0:
                rim_start(n_rim)
            kept = min(begin + n, grads.shape[0]) - begin
            if kept > 0:
                grads[pl.ds(begin, kept)] = grad[:kept]

        return sink

    def last(begin, n, grad):
        g0[pl.ds(begin, n)] = grad

    rim_wait(2)
    backward(2, d2, (6, 5), g2, hand_on(d1, 2, s1, g1, 3))
    clear(d1, 2)
    rim_wait(3)
    backward(1, d1, (5, 4), g1, hand_on(d0, 1, s0, g0, 4))
    clear(d0, 1)
    rim_wait(4)
    backward(0, d0, (8,), g0, last)

    def v_of(u):
        return (1 - half) * (7 - u) + half * u

    spread[...] = jnp.zeros(spread.shape, F32)
    for t in range(8 + Q - 1):
        total = sum(g0[v_of(t - q), q] for q in range(Q) if 0 <= t - q < 8)
        place = pl.ds(8 + t, 16, stride=Q)
        for c in range(2):
            spread[c, place, :] = spread[c, place, :] + total[:, 128 * c : 128 * c + 128]

    def rg_source(k, chan):
        return spread.at[chan, pl.ds(pl.multiple_of(8 - 8 * half + 16 * k, 8), 16)]

    def rg_copy(k, chan):
        return send(rg_source(k, chan), rg.at[k, half], rg_ss.at[k, chan], rg_rs.at[k, half], k, chan)

    def each_rg(act):
        for k in (4, 3, 2, 1, 0):
            if k == 0:
                act(rg_copy(0, mate))
            else:
                @pl.when(there(k))
                def _(k=k):
                    for chan in range(2):
                        act(rg_copy(k, chan))

    each_rg(lambda c: c.start())
    lg = jnp.concatenate(
        [jnp.sum(g0[v_of(u)].reshape(64, 256), axis=0, keepdims=True) for u in range(8)], axis=0
    )
    low, high = lg[:, :128], lg[:, 128:]
    swap_out[0:8] = jnp.where(half == 0, high, low)
    swap_out[8:16] = contact
    swap_copy = send(swap_out, swap, swap_ss.at[0], swap_rs.at[0], 0, mate)
    swap_copy.start()
    rg[0, half] = spread[half, pl.ds(pl.multiple_of(8 - 8 * half, 8), 16), :]
    mine = pl.ds(pl.multiple_of(8 * half, 8), 8)
    other = pl.ds(pl.multiple_of(8 * mate, 8), 8)
    lg_out[mine, :] = jnp.where(half == 0, low, high)
    contact_out[mine, :] = contact[:, :64]

    for k in range(1, 5):
        @pl.when(jnp.logical_not(there(-k)))
        def _(k=k):
            rg[k] = jnp.zeros(rg.shape[1:], F32)

    swap_copy.wait_recv()
    lg_out[other, :] = swap[0:8]
    contact_out[other, :] = swap[8:16, :64]

    def rg_wait(k, chan):
        send(rg_source(k, chan), rg.at[k, chan], rg_ss.at[k, chan], rg_rs.at[k, chan], 0, mate).wait_recv()

    for k in range(5):
        if k == 0:
            rg_wait(0, mate)
        else:
            @pl.when(there(-k))
            def _(k=k):
                for chan in range(2):
                    rg_wait(k, chan)
    rg_out[...] = sum(rg[k, c] for k in range(5) for c in range(2))

    each_emb(lambda c: c.wait_send())
    for k in range(layers):
        w_copy(k).wait_send()
    ro_copy.wait_send()
    each_cot(lambda c: c.wait_send())
    each_rg(lambda c: c.wait_send())
    swap_copy.wait_send()
    for copies in rims:
        for copy in copies:
            copy.wait_send()


def hand_out(*refs):
    sems = refs[6]
    copies = [pltpu.make_async_copy(refs[n], refs[3 + n], sems.at[n]) for n in range(3)]
    for copy in copies:
        copy.start()
    for copy in copies:
        copy.wait()


def local(slabs, left_embed, right_embed, conv_weight, readout, cotangent):
    vmem = pl.BlockSpec(memory_space=pltpu.VMEM)
    anywhere = pl.BlockSpec(memory_space=pl.ANY)
    dma = pltpu.SemaphoreType.DMA

    def padded(rows, r):
        return pltpu.VMEM((rows, Q + 2 * r, 16, 256), BF16)

    def wide(rows):
        return pltpu.VMEM((rows, Q, 16, 256), F32)

    out_shape = (
        jax.ShapeDtypeStruct((16, 64), F32),
        jax.ShapeDtypeStruct((16, 128), F32),
        jax.ShapeDtypeStruct((16, 128), F32),
    )
    results = pl.pallas_call(
        functools.partial(kernel, slabs),
        out_shape=out_shape,
        in_specs=[vmem, vmem, anywhere, vmem, vmem],
        out_specs=(vmem, vmem, vmem),
        scratch_shapes=[
            pltpu.VMEM((32, 128), BF16),
            pltpu.VMEM((7, 2, 32, 128), BF16),
            pltpu.VMEM((4, 112, 128), F32),
            pltpu.VMEM((2, 3, 3, 3, 256, 128), BF16),
            pltpu.VMEM((48, 128), F32),
            pltpu.VMEM((2, 8, 128), F32),
            padded(23, 1), padded(23, 2), padded(23, 4),
            padded(19, 4), padded(13, 2), padded(10, 1),
            wide(9), wide(11), wide(11), wide(9), wide(8),
            pltpu.VMEM((2, 88, 128), F32),
            pltpu.VMEM((5, 2, 16, 128), F32),
            pltpu.VMEM((16, 128), F32),
            pltpu.VMEM((16, 128), F32),
            dma((7, 2)), dma((7, 2)), dma((3,)), dma((3,)), dma((3,)),
            dma((2,)), dma((2,)), dma((1,)), dma((1,)),
            dma((5, 2)), dma((5, 2)), dma((1,)), dma((1,)),
            dma((5, 4)), dma((5, 4)),
        ],
        compiler_params=pltpu.CompilerParams(
            collective_id=0, has_side_effects=True, vmem_limit_bytes=56 * 2**20
        ),
        cost_estimate=pl.CostEstimate(flops=8 * 10**9, bytes_accessed=4 * 10**6, transcendentals=10**6),
    )(left_embed, right_embed, conv_weight, readout.reshape(1, 128), cotangent)
    return pl.pallas_call(
        hand_out, out_shape=out_shape, in_specs=[anywhere] * 3, out_specs=(anywhere,) * 3,
        scratch_shapes=[dma((3,))],
    )(*results)


def solution(mesh):
    return jax.shard_map(
        functools.partial(local, mesh.shape["chrom"]),
        mesh=mesh,
        in_specs=(
            P("chrom", "chan"),
            P("chrom", "chan"),
            P(None, None, None, None, "chan"),
            P("chan"),
            P("chrom", None),
        ),
        out_specs=(P("chrom", None), P("chrom", "chan"), P("chrom", "chan")),
        check_vma=False,
    )
```

```python
import functools

import jax
import jax.numpy as jnp
from jax import lax
from jax.experimental import pallas as pl
from jax.experimental.pallas import tpu as pltpu
from jax.sharding import PartitionSpec as P

MESH = pl.DeviceIdType.MESH
F32, BF16 = jnp.float32, jnp.bfloat16
BACK, AHEAD = 1, 5
Q = 4


def split3(x):
    hi = x.astype(BF16)
    rest = x - hi.astype(F32)
    mid = rest.astype(BF16)
    return hi, mid, (rest - mid.astype(F32)).astype(BF16)


def nt(a, b):
    return lax.dot_general(a, b, (((1,), (1,)), ((), ())), preferred_element_type=F32)


def shifted(x, step):
    n = x.shape[2]
    flat = x.reshape((x.shape[0] * x.shape[1],) + x.shape[2:])
    moved = pltpu.roll(flat, step % n, 1)
    where = lax.broadcasted_iota(jnp.int32, flat.shape, 1)
    edge = 0 if step == 1 else n - 1
    return jnp.where(where == edge, 0.0, moved).reshape(x.shape)


def put(buf, row, x, r):
    rows = pl.ds(row, x.shape[0])
    buf[rows, r : r + Q] = x.astype(BF16)
    buf[rows, 0:r] = shifted(x[:, Q - r :], 1).astype(BF16)
    buf[rows, r + Q :] = shifted(x[:, :r], -1).astype(BF16)


def kernel(
    slabs,
    left_ref, right_ref, w_hbm, ro_ref, cot_ref,
    contact_out, lg_out, rg_out,
    block, emb, rwin, w, cot, ro, p0, p1, p2, d2, d1, d0, s0, s1, g2, g1, g0, columns, p3,
    spread, rg, swap_out, swap,
    emb_ss, emb_rs, w_ls, w_ss, w_rs, cot_ss, cot_rs, ro_ss, ro_rs, rg_ss, rg_rs, swap_ss, swap_rs, rim_ss, rim_rs,
):
    slab = lax.axis_index("chrom")
    half = lax.axis_index("chan")
    mate = 1 - half

    def there(delta):
        return jnp.logical_and(slab + delta >= 0, slab + delta < slabs)

    def send(src, dst, ss, rs, delta, chan):
        return pltpu.make_async_remote_copy(
            src_ref=src, dst_ref=dst, send_sem=ss, recv_sem=rs,
            device_id=(slab + delta, chan), device_id_type=MESH,
        )

    barrier = pltpu.get_barrier_semaphore()
    reach = max(BACK, AHEAD)
    for delta in range(-reach, reach + 1):
        if delta == 0:
            pl.semaphore_signal(barrier, inc=1, device_id=(slab, mate), device_id_type=MESH)
        else:
            @pl.when(there(delta))
            def _(delta=delta):
                for chan in range(2):
                    pl.semaphore_signal(barrier, inc=1, device_id=(slab + delta, chan), device_id_type=MESH)

    layers = w.shape[1]
    local = [pltpu.make_async_copy(w_hbm.at[k], w.at[half, k], w_ls.at[k]) for k in range(layers)]
    for copy in local:
        copy.start()
    block[0:16] = right_ref[...]
    block[16:32] = left_ref[...]
    emb[BACK, half] = block[...]
    cot[16:32] = jnp.concatenate([cot_ref[...], jnp.zeros((16, 64), F32)], axis=1)
    ro[half] = jnp.broadcast_to(ro_ref[...], (8, 128))
    for k in range(BACK + AHEAD + 1):
        if k != BACK:
            @pl.when(jnp.logical_not(there(k - BACK)))
            def _(k=k):
                emb[k] = jnp.zeros(emb.shape[1:], BF16)
    for delta in (-1, 1):
        @pl.when(jnp.logical_not(there(delta)))
        def _(delta=delta):
            cot[16 + 16 * delta : 32 + 16 * delta] = jnp.zeros((16, 128), F32)

    pl.semaphore_wait(
        barrier, 2 * (jnp.minimum(slab, reach) + jnp.minimum(slabs - 1 - slab, reach) + 1) - 1
    )

    def emb_copy(delta, chan):
        k = BACK - delta
        return send(block, emb.at[k, half], emb_ss.at[k, chan], emb_rs.at[k, half], delta, chan)

    def each_emb(act):
        for delta in (0, 1, -1, -2, -3, -4, -5):
            if delta == 0:
                act(emb_copy(0, mate))
            else:
                @pl.when(there(delta))
                def _(delta=delta):
                    for chan in range(2):
                        act(emb_copy(delta, chan))

    def w_copy(k):
        return send(w_hbm.at[k], w.at[half, k], w_ss.at[k], w_rs.at[k], 0, mate)

    def cot_copy(delta):
        place = pl.ds(16 - 16 * delta, 16)
        slot = (1 - delta) // 2
        return send(cot.at[pl.ds(16, 16)], cot.at[place], cot_ss.at[slot], cot_rs.at[slot], delta, half)

    def each_cot(act):
        for delta in (-1, 1):
            @pl.when(there(delta))
            def _(delta=delta):
                act(cot_copy(delta))

    ro_copy = send(ro.at[half], ro.at[half], ro_ss.at[0], ro_rs.at[0], 0, mate)

    each_emb(lambda c: c.start())
    for k in range(layers):
        w_copy(k).start()
    ro_copy.start()
    each_cot(lambda c: c.start())

    def emb_wait(k, chan):
        send(block, emb.at[k, chan], emb_ss.at[k, chan], emb_rs.at[k, chan], 0, mate).wait_recv()

    for k in range(BACK + AHEAD + 1):
        if k == BACK:
            emb_wait(k, mate)
        else:
            @pl.when(there(k - BACK))
            def _(k=k):
                for chan in range(2):
                    emb_wait(k, chan)

    for k in range(BACK + AHEAD + 1):
        for c in range(2):
            rwin[c, 16 * k : 16 * k + 16] = emb[k, c, 0:16].astype(F32)
            if k < 3:
                rwin[2 + c, 16 * k : 16 * k + 16] = emb[k, c, 16:32].astype(F32)

    sign = 2 * half - 1

    def bin_of(v):
        return 7 + half + sign * v

    outer_edge = jnp.logical_or(
        jnp.logical_and(half == 0, slab == 0), jnp.logical_and(half == 1, slab == slabs - 1)
    )

    def clear(buf, r):
        @pl.when(outer_edge)
        def _():
            buf[r + 8 :] = jnp.zeros((buf.shape[0] - r - 8,) + buf.shape[1:], BF16)

    def rim(n, buf, r):
        return [
            send(buf.at[r + j], buf.at[r - 1 - j], rim_ss.at[n, j], rim_rs.at[n, j], 0, mate)
            for j in range(r)
        ]

    rims = [rim(n, buf, r) for n, (buf, r) in enumerate([(p1, 2), (p2, 4), (d2, 4), (d1, 2), (d0, 1)])]

    def rim_start(n):
        for copy in rims[n]:
            copy.start()

    def rim_wait(n):
        for copy in rims[n]:
            copy.wait_recv()

    def first_pair(row, unused):
        place = 16 + bin_of(row - 1)
        left = jnp.concatenate([rwin[2 + c, pl.ds(place, 1), :] for c in range(2)], axis=1)
        tiles = [
            left + jnp.concatenate([rwin[c, pl.ds(place + q, 16, stride=Q), :] for c in range(2)], axis=1)
            for q in range(Q)
        ]
        put(p0, row, jnp.stack(tiles)[None], 1)
        return unused

    lax.fori_loop(0, 23, first_pair, 0)
    clear(p0, 1)

    taps = [2 - 2 * half, 1, 2 * half]

    def weights(k):
        local[k].wait()
        send(w_hbm.at[k], w.at[mate, k], w_ss.at[k], w_rs.at[k], 0, mate).wait_recv()

    def forward(k, src, steps, n, sink):
        r = 2**k
        weights(k)

        def step(index, unused):
            begin = index * n
            wide = jnp.concatenate(
                [jnp.concatenate([w[c, k, a].reshape(3 * 256, 128) for a in taps], axis=0) for c in range(2)],
                axis=1,
            )
            lhs = jnp.concatenate(
                [
                    src[pl.ds(begin + m * r, n), b * r : b * r + Q].reshape(n * 64, 256)
                    for m in range(3) for b in range(3)
                ],
                axis=1,
            )
            z = jnp.dot(lhs, wide, preferred_element_type=F32).reshape(n, Q, 16, 256)
            s = 0.5 + 0.5 * jnp.tanh(0.5 * z)
            old = src[pl.ds(begin + r, n), r : r + Q].astype(F32)
            zs = z * s
            sink(index, begin, n, old + zs, s + zs * (1.0 - s))
            return unused

        lax.fori_loop(0, steps, step, 0)

    def rim_after(index, n_rim):
        @pl.when(index == 0)
        def _():
            rim_start(n_rim)

    def keep(buf, r, slopes, n_rim):
        def sink(index, begin, n, x, slope):
            put(buf, begin + r, x, r)
            rim_after(index, n_rim)
            slopes[pl.ds(begin, n)] = slope

        return sink

    forward(0, p0, 3, 7, keep(p1, 2, s0, 0))
    clear(p1, 2)
    rim_wait(0)
    forward(1, p1, 4, 5, keep(p2, 4, s1, 1))
    clear(p2, 4)

    n_i = lax.broadcasted_iota(jnp.int32, (64, 128), 0)
    d_i = lax.broadcasted_iota(jnp.int32, (64, 128), 1)
    order = jnp.where(d_i == Q * (n_i % 16) + n_i // 16, 1.0, 0.0).astype(BF16)

    send(ro.at[half], ro.at[mate], ro_ss.at[0], ro_rs.at[0], 0, mate).wait_recv()
    for delta in (-1, 1):
        @pl.when(there(delta))
        def _(delta=delta):
            slot = (1 + delta) // 2
            send(
                cot.at[pl.ds(16, 16)], cot.at[pl.ds(16 + 16 * delta, 16)],
                cot_ss.at[slot], cot_rs.at[slot], delta, half,
            ).wait_recv()
    readout = jnp.concatenate([ro[0, 0:1], ro[1, 0:1]], axis=1)
    parts = split3(readout)
    row_i = lax.broadcasted_iota(jnp.int32, (16, 256), 0)
    ro_rows = sum(
        jnp.where(row_i == m, jnp.broadcast_to(part.astype(F32), (16, 256)), 0.0) for m, part in enumerate(parts)
    ).astype(BF16)
    cot_win = jnp.concatenate([cot[pl.ds(16 + bin_of(v), 1), :] for v in range(16)], axis=0)
    cot_t = sum(nt(order, part) for part in split3(cot_win))

    for v in range(16):
        columns[v] = jnp.broadcast_to(cot_t[:, v : v + 1], (64, 128))

    def last_sink(index, begin, n, x, slope):
        column = columns[pl.ds(begin, n)]
        grad = jnp.concatenate([column, column], axis=2) * readout[None]
        grad = grad.reshape(n, Q, 16, 256)
        put(d2, begin + 4, grad * slope, 4)
        rim_after(index, 2)
        g2[pl.ds(begin, n)] = grad
        p3[pl.ds(begin, n)] = x.astype(BF16)

    rim_wait(1)
    forward(2, p2, 3, 5, last_sink)
    clear(d2, 4)
    contacts = [
        jnp.sum(nt(ro_rows, p3[v].reshape(64, 256)), axis=0, keepdims=True) for v in range(8)
    ]
    outwards = jnp.concatenate(contacts, axis=0)
    inwards = jnp.concatenate(contacts[::-1], axis=0)
    contact_rows = jnp.where(half == 1, outwards, inwards)
    contact = sum(jnp.dot(part, order, preferred_element_type=F32) for part in split3(contact_rows))

    def backward(k, src, steps, n, before, sink):
        r = 2**k

        def step(index, unused):
            begin = index * n
            wide = jnp.concatenate([w[c, k, a, b] for a in taps for b in range(3) for c in range(2)], axis=1)
            lhs = jnp.concatenate(
                [
                    src[pl.ds(begin + (2 - m) * r, n), (2 - b) * r : (2 - b) * r + Q].reshape(n * 64, 256)
                    for m in range(3) for b in range(3)
                ],
                axis=1,
            )
            sink(index, begin, n, before[pl.ds(begin, n)] + nt(lhs, wide).reshape(n, Q, 16, 256))
            return unused

        lax.fori_loop(0, steps, step, 0)

    def hand_on(buf, r, slopes, grads, n_rim):
        def sink(index, begin, n, grad):
            put(buf, begin + r, grad * slopes[pl.ds(begin, n)], r)
            rim_after(index, n_rim)
            grads[pl.ds(begin, n)] = grad

        return sink

    def last(index, begin, n, grad):
        g0[pl.ds(begin, n)] = grad

    rim_wait(2)
    backward(2, d2, 2, 6, g2, hand_on(d1, 2, s1, g1, 3))
    clear(d1, 2)
    rim_wait(3)
    backward(1, d1, 2, 5, g1, hand_on(d0, 1, s0, g0, 4))
    clear(d0, 1)
    rim_wait(4)
    backward(0, d0, 2, 4, g0, last)

    def v_of(u):
        return (1 - half) * (7 - u) + half * u

    spread[...] = jnp.zeros(spread.shape, F32)
    for t in range(8 + Q - 1):
        total = sum(g0[v_of(t - q), q] for q in range(Q) if 0 <= t - q < 8)
        place = pl.ds(8 + t, 16, stride=Q)
        for c in range(2):
            spread[c, place, :] = spread[c, place, :] + total[:, 128 * c : 128 * c + 128]

    def rg_source(k, chan):
        return spread.at[chan, pl.ds(pl.multiple_of(8 - 8 * half + 16 * k, 8), 16)]

    def rg_copy(k, chan):
        return send(rg_source(k, chan), rg.at[k, half], rg_ss.at[k, chan], rg_rs.at[k, half], k, chan)

    def each_rg(act):
        for k in (4, 3, 2, 1, 0):
            if k == 0:
                act(rg_copy(0, mate))
            else:
                @pl.when(there(k))
                def _(k=k):
                    for chan in range(2):
                        act(rg_copy(k, chan))

    each_rg(lambda c: c.start())
    lg = jnp.concatenate(
        [jnp.sum(g0[v_of(u)].reshape(64, 256), axis=0, keepdims=True) for u in range(8)], axis=0
    )
    low, high = lg[:, :128], lg[:, 128:]
    swap_out[0:8] = jnp.where(half == 0, high, low)
    swap_out[8:16] = contact
    swap_copy = send(swap_out, swap, swap_ss.at[0], swap_rs.at[0], 0, mate)
    swap_copy.start()
    rg[0, half] = spread[half, pl.ds(pl.multiple_of(8 - 8 * half, 8), 16), :]
    mine = pl.ds(pl.multiple_of(8 * half, 8), 8)
    other = pl.ds(pl.multiple_of(8 * mate, 8), 8)
    lg_out[mine, :] = jnp.where(half == 0, low, high)
    contact_out[mine, :] = contact[:, :64]

    for k in range(1, 5):
        @pl.when(jnp.logical_not(there(-k)))
        def _(k=k):
            rg[k] = jnp.zeros(rg.shape[1:], F32)

    swap_copy.wait_recv()
    lg_out[other, :] = swap[0:8]
    contact_out[other, :] = swap[8:16, :64]

    def rg_wait(k, chan):
        send(rg_source(k, chan), rg.at[k, chan], rg_ss.at[k, chan], rg_rs.at[k, chan], 0, mate).wait_recv()

    for k in range(5):
        if k == 0:
            rg_wait(0, mate)
        else:
            @pl.when(there(-k))
            def _(k=k):
                for chan in range(2):
                    rg_wait(k, chan)
    rg_out[...] = sum(rg[k, c] for k in range(5) for c in range(2))

    each_emb(lambda c: c.wait_send())
    for k in range(layers):
        w_copy(k).wait_send()
    ro_copy.wait_send()
    each_cot(lambda c: c.wait_send())
    each_rg(lambda c: c.wait_send())
    swap_copy.wait_send()
    for copies in rims:
        for copy in copies:
            copy.wait_send()


def hand_out(*refs):
    sems = refs[6]
    copies = [pltpu.make_async_copy(refs[n], refs[3 + n], sems.at[n]) for n in range(3)]
    for copy in copies:
        copy.start()
    for copy in copies:
        copy.wait()


def local(slabs, left_embed, right_embed, conv_weight, readout, cotangent):
    vmem = pl.BlockSpec(memory_space=pltpu.VMEM)
    anywhere = pl.BlockSpec(memory_space=pl.ANY)
    dma = pltpu.SemaphoreType.DMA

    def padded(rows, r):
        return pltpu.VMEM((rows, Q + 2 * r, 16, 256), BF16)

    def wide(rows):
        return pltpu.VMEM((rows, Q, 16, 256), F32)

    out_shape = (
        jax.ShapeDtypeStruct((16, 64), F32),
        jax.ShapeDtypeStruct((16, 128), F32),
        jax.ShapeDtypeStruct((16, 128), F32),
    )
    results = pl.pallas_call(
        functools.partial(kernel, slabs),
        out_shape=out_shape,
        in_specs=[vmem, vmem, anywhere, vmem, vmem],
        out_specs=(vmem, vmem, vmem),
        scratch_shapes=[
            pltpu.VMEM((32, 128), BF16),
            pltpu.VMEM((7, 2, 32, 128), BF16),
            pltpu.VMEM((4, 112, 128), F32),
            pltpu.VMEM((2, 3, 3, 3, 256, 128), BF16),
            pltpu.VMEM((48, 128), F32),
            pltpu.VMEM((2, 8, 128), F32),
            padded(23, 1), padded(24, 2), padded(24, 4),
            padded(20, 4), padded(14, 2), padded(11, 1),
            wide(21), wide(20), wide(15), wide(12), wide(10),
            pltpu.VMEM((16, 64, 128), F32), pltpu.VMEM((15, Q, 16, 256), BF16),
            pltpu.VMEM((2, 88, 128), F32),
            pltpu.VMEM((5, 2, 16, 128), F32),
            pltpu.VMEM((16, 128), F32),
            pltpu.VMEM((16, 128), F32),
            dma((7, 2)), dma((7, 2)), dma((3,)), dma((3,)), dma((3,)),
            dma((2,)), dma((2,)), dma((1,)), dma((1,)),
            dma((5, 2)), dma((5, 2)), dma((1,)), dma((1,)),
            dma((5, 4)), dma((5, 4)),
        ],
        compiler_params=pltpu.CompilerParams(
            collective_id=0, has_side_effects=True, vmem_limit_bytes=56 * 2**20
        ),
        cost_estimate=pl.CostEstimate(flops=8 * 10**9, bytes_accessed=4 * 10**6, transcendentals=10**6),
    )(left_embed, right_embed, conv_weight, readout.reshape(1, 128), cotangent)
    return pl.pallas_call(
        hand_out, out_shape=out_shape, in_specs=[anywhere] * 3, out_specs=(anywhere,) * 3,
        scratch_shapes=[dma((3,))],
    )(*results)


def solution(mesh):
    return jax.shard_map(
        functools.partial(local, mesh.shape["chrom"]),
        mesh=mesh,
        in_specs=(
            P("chrom", "chan"),
            P("chrom", "chan"),
            P(None, None, None, None, "chan"),
            P("chan"),
            P("chrom", None),
        ),
        out_specs=(P("chrom", None), P("chrom", "chan"), P("chrom", "chan")),
        check_vma=False,
    )
```

```python
import functools

import jax
import jax.numpy as jnp
from jax import lax
from jax.experimental import pallas as pl
from jax.experimental.pallas import tpu as pltpu
from jax.sharding import PartitionSpec as P

MESH = pl.DeviceIdType.MESH
F32, BF16 = jnp.float32, jnp.bfloat16
BACK, AHEAD = 1, 5
Q = 4


def split3(x):
    hi = x.astype(BF16)
    rest = x - hi.astype(F32)
    mid = rest.astype(BF16)
    return hi, mid, (rest - mid.astype(F32)).astype(BF16)


def nt(a, b):
    return lax.dot_general(a, b, (((1,), (1,)), ((), ())), preferred_element_type=F32)


def shifted(x, step):
    n = x.shape[2]
    flat = x.reshape((x.shape[0] * x.shape[1],) + x.shape[2:])
    moved = pltpu.roll(flat, step % n, 1)
    where = lax.broadcasted_iota(jnp.int32, flat.shape, 1)
    edge = 0 if step == 1 else n - 1
    return jnp.where(where == edge, 0.0, moved).reshape(x.shape)


def put(buf, row, x, r):
    rows = pl.ds(row, x.shape[0])
    buf[rows, r : r + Q] = x.astype(BF16)
    buf[rows, 0:r] = shifted(x[:, Q - r :], 1).astype(BF16)
    buf[rows, r + Q :] = shifted(x[:, :r], -1).astype(BF16)


def kernel(
    slabs,
    left_ref, right_ref, w_hbm, ro_ref, cot_ref,
    contact_out, lg_out, rg_out,
    block, emb, rwin, w, cot, ro, p0, p1, p2, d2, d1, d0, s0, s1, g2, g1, g0, columns, p3,
    spread, rg, swap_out, swap,
    emb_ss, emb_rs, w_ls, w_ss, w_rs, cot_ss, cot_rs, ro_ss, ro_rs, rg_ss, rg_rs, swap_ss, swap_rs, rim_ss, rim_rs,
):
    slab = lax.axis_index("chrom")
    half = lax.axis_index("chan")
    mate = 1 - half

    def there(delta):
        return jnp.logical_and(slab + delta >= 0, slab + delta < slabs)

    def send(src, dst, ss, rs, delta, chan):
        return pltpu.make_async_remote_copy(
            src_ref=src, dst_ref=dst, send_sem=ss, recv_sem=rs,
            device_id=(slab + delta, chan), device_id_type=MESH,
        )

    barrier = pltpu.get_barrier_semaphore()
    reach = max(BACK, AHEAD)
    for delta in range(-reach, reach + 1):
        if delta == 0:
            pl.semaphore_signal(barrier, inc=1, device_id=(slab, mate), device_id_type=MESH)
        else:
            @pl.when(there(delta))
            def _(delta=delta):
                for chan in range(2):
                    pl.semaphore_signal(barrier, inc=1, device_id=(slab + delta, chan), device_id_type=MESH)

    layers = w.shape[1]
    local = [pltpu.make_async_copy(w_hbm.at[k], w.at[half, k], w_ls.at[k]) for k in range(layers)]
    for copy in local:
        copy.start()
    block[0:16] = right_ref[...]
    block[16:32] = left_ref[...]
    emb[BACK, half] = block[...]
    cot[16:32] = jnp.concatenate([cot_ref[...], jnp.zeros((16, 64), F32)], axis=1)
    ro[half] = jnp.broadcast_to(ro_ref[...], (8, 128))
    for k in range(BACK + AHEAD + 1):
        if k != BACK:
            @pl.when(jnp.logical_not(there(k - BACK)))
            def _(k=k):
                emb[k] = jnp.zeros(emb.shape[1:], BF16)
    for delta in (-1, 1):
        @pl.when(jnp.logical_not(there(delta)))
        def _(delta=delta):
            cot[16 + 16 * delta : 32 + 16 * delta] = jnp.zeros((16, 128), F32)

    pl.semaphore_wait(
        barrier, 2 * (jnp.minimum(slab, reach) + jnp.minimum(slabs - 1 - slab, reach) + 1) - 1
    )

    def emb_copy(delta, chan):
        k = BACK - delta
        return send(block, emb.at[k, half], emb_ss.at[k, chan], emb_rs.at[k, half], delta, chan)

    def each_emb(act):
        for delta in (0, 1, -1, -2, -3, -4, -5):
            if delta == 0:
                act(emb_copy(0, mate))
            else:
                @pl.when(there(delta))
                def _(delta=delta):
                    for chan in range(2):
                        act(emb_copy(delta, chan))

    def w_copy(k, a):
        return send(w_hbm.at[k, a], w.at[half, k, a], w_ss.at[k, a], w_rs.at[k, a], 0, mate)

    every_w = [(k, a) for k in range(layers) for a in range(3)]

    def cot_copy(delta):
        place = pl.ds(16 - 16 * delta, 16)
        slot = (1 - delta) // 2
        return send(cot.at[pl.ds(16, 16)], cot.at[place], cot_ss.at[slot], cot_rs.at[slot], delta, half)

    def each_cot(act):
        for delta in (-1, 1):
            @pl.when(there(delta))
            def _(delta=delta):
                act(cot_copy(delta))

    ro_copy = send(ro.at[half], ro.at[half], ro_ss.at[0], ro_rs.at[0], 0, mate)

    each_emb(lambda c: c.start())
    for k, a in every_w:
        w_copy(k, a).start()
    ro_copy.start()
    each_cot(lambda c: c.start())

    def emb_wait(k, chan):
        send(block, emb.at[k, chan], emb_ss.at[k, chan], emb_rs.at[k, chan], 0, mate).wait_recv()

    for k in range(BACK + AHEAD + 1):
        if k == BACK:
            emb_wait(k, mate)
        else:
            @pl.when(there(k - BACK))
            def _(k=k):
                for chan in range(2):
                    emb_wait(k, chan)

    for k in range(BACK + AHEAD + 1):
        for c in range(2):
            rwin[c, 16 * k : 16 * k + 16] = emb[k, c, 0:16].astype(F32)
            if k < 3:
                rwin[2 + c, 16 * k : 16 * k + 16] = emb[k, c, 16:32].astype(F32)

    sign = 2 * half - 1

    def bin_of(v):
        return 7 + half + sign * v

    outer_edge = jnp.logical_or(
        jnp.logical_and(half == 0, slab == 0), jnp.logical_and(half == 1, slab == slabs - 1)
    )

    def clear(buf, r):
        @pl.when(outer_edge)
        def _():
            buf[r + 8 :] = jnp.zeros((buf.shape[0] - r - 8,) + buf.shape[1:], BF16)

    def rim(n, buf, r):
        return [
            send(buf.at[r + j], buf.at[r - 1 - j], rim_ss.at[n, j], rim_rs.at[n, j], 0, mate)
            for j in range(r)
        ]

    rims = [rim(n, buf, r) for n, (buf, r) in enumerate([(p1, 2), (p2, 4), (d2, 4), (d1, 2), (d0, 1)])]

    def rim_start(n):
        for copy in rims[n]:
            copy.start()

    def rim_wait(n):
        for copy in rims[n]:
            copy.wait_recv()

    def first_pair(row, unused):
        place = 16 + bin_of(row - 1)
        left = jnp.concatenate([rwin[2 + c, pl.ds(place, 1), :] for c in range(2)], axis=1)
        tiles = [
            left + jnp.concatenate([rwin[c, pl.ds(place + q, 16, stride=Q), :] for c in range(2)], axis=1)
            for q in range(Q)
        ]
        put(p0, row, jnp.stack(tiles)[None], 1)
        return unused

    lax.fori_loop(0, 24, first_pair, 0)
    clear(p0, 1)

    taps = [2 - 2 * half, 1, 2 * half]

    def weights(k):
        local[k].wait()
        for a in range(3):
            send(w_hbm.at[k, a], w.at[mate, k, a], w_ss.at[k, a], w_rs.at[k, a], 0, mate).wait_recv()

    def forward(k, src, steps, n, sink):
        r = 2**k
        weights(k)

        def step(index, unused):
            begin = index * n
            wide = jnp.concatenate(
                [jnp.concatenate([w[c, k, a].reshape(3 * 256, 128) for a in taps], axis=0) for c in range(2)],
                axis=1,
            )
            lhs = jnp.concatenate(
                [
                    src[pl.ds(begin + m * r, n), b * r : b * r + Q].reshape(n * 64, 256)
                    for m in range(3) for b in range(3)
                ],
                axis=1,
            )
            z = jnp.dot(lhs, wide, preferred_element_type=F32).reshape(n, Q, 16, 256)
            s = 0.5 + 0.5 * jnp.tanh(0.5 * z)
            old = src[pl.ds(begin + r, n), r : r + Q].astype(F32)
            zs = z * s
            sink(index, begin, n, old + zs, s + zs * (1.0 - s))
            return unused

        lax.fori_loop(0, steps, step, 0)

    def rim_after(index, n_rim):
        @pl.when(index == 0)
        def _():
            rim_start(n_rim)

    def keep(buf, r, slopes, n_rim):
        def sink(index, begin, n, x, slope):
            put(buf, begin + r, x, r)
            rim_after(index, n_rim)
            slopes[pl.ds(begin, n)] = slope

        return sink

    forward(0, p0, 2, 11, keep(p1, 2, s0, 0))
    clear(p1, 2)
    rim_wait(0)
    forward(1, p1, 2, 10, keep(p2, 4, s1, 1))
    clear(p2, 4)

    n_i = lax.broadcasted_iota(jnp.int32, (64, 128), 0)
    d_i = lax.broadcasted_iota(jnp.int32, (64, 128), 1)
    order = jnp.where(d_i == Q * (n_i % 16) + n_i // 16, 1.0, 0.0).astype(BF16)

    send(ro.at[half], ro.at[mate], ro_ss.at[0], ro_rs.at[0], 0, mate).wait_recv()
    for delta in (-1, 1):
        @pl.when(there(delta))
        def _(delta=delta):
            slot = (1 + delta) // 2
            send(
                cot.at[pl.ds(16, 16)], cot.at[pl.ds(16 + 16 * delta, 16)],
                cot_ss.at[slot], cot_rs.at[slot], delta, half,
            ).wait_recv()
    readout = jnp.concatenate([ro[0, 0:1], ro[1, 0:1]], axis=1)
    parts = split3(readout)
    row_i = lax.broadcasted_iota(jnp.int32, (16, 256), 0)
    ro_rows = sum(
        jnp.where(row_i == m, jnp.broadcast_to(part.astype(F32), (16, 256)), 0.0) for m, part in enumerate(parts)
    ).astype(BF16)
    cot_win = jnp.concatenate([cot[pl.ds(16 + bin_of(v), 1), :] for v in range(16)], axis=0)
    cot_t = sum(nt(order, part) for part in split3(cot_win))

    for v in range(16):
        columns[v] = jnp.broadcast_to(cot_t[:, v : v + 1], (64, 128))

    def last_sink(index, begin, n, x, slope):
        column = columns[pl.ds(begin, n)]
        grad = jnp.concatenate([column, column], axis=2) * readout[None]
        grad = grad.reshape(n, Q, 16, 256)
        put(d2, begin + 4, grad * slope, 4)
        rim_after(index, 2)
        g2[pl.ds(begin, n)] = grad
        p3[pl.ds(begin, n)] = x.astype(BF16)

    rim_wait(1)
    forward(2, p2, 2, 8, last_sink)
    clear(d2, 4)
    contacts = [
        jnp.sum(nt(ro_rows, p3[v].reshape(64, 256)), axis=0, keepdims=True) for v in range(8)
    ]
    outwards = jnp.concatenate(contacts, axis=0)
    inwards = jnp.concatenate(contacts[::-1], axis=0)
    contact_rows = jnp.where(half == 1, outwards, inwards)
    contact = sum(jnp.dot(part, order, preferred_element_type=F32) for part in split3(contact_rows))

    def backward(k, src, steps, n, before, sink):
        r = 2**k

        def step(index, unused):
            begin = index * n
            wide = jnp.concatenate([w[c, k, a, b] for a in taps for b in range(3) for c in range(2)], axis=1)
            lhs = jnp.concatenate(
                [
                    src[pl.ds(begin + (2 - m) * r, n), (2 - b) * r : (2 - b) * r + Q].reshape(n * 64, 256)
                    for m in range(3) for b in range(3)
                ],
                axis=1,
            )
            sink(index, begin, n, before[pl.ds(begin, n)] + nt(lhs, wide).reshape(n, Q, 16, 256))
            return unused

        lax.fori_loop(0, steps, step, 0)

    def hand_on(buf, r, slopes, grads, n_rim):
        def sink(index, begin, n, grad):
            put(buf, begin + r, grad * slopes[pl.ds(begin, n)], r)
            rim_after(index, n_rim)
            grads[pl.ds(begin, n)] = grad

        return sink

    def last(index, begin, n, grad):
        g0[pl.ds(begin, n)] = grad

    rim_wait(2)
    backward(2, d2, 2, 6, g2, hand_on(d1, 2, s1, g1, 3))
    clear(d1, 2)
    rim_wait(3)
    backward(1, d1, 2, 5, g1, hand_on(d0, 1, s0, g0, 4))
    clear(d0, 1)
    rim_wait(4)
    backward(0, d0, 1, 8, g0, last)

    def v_of(u):
        return (1 - half) * (7 - u) + half * u

    spread[...] = jnp.zeros(spread.shape, F32)
    for t in range(8 + Q - 1):
        total = sum(g0[v_of(t - q), q] for q in range(Q) if 0 <= t - q < 8)
        place = pl.ds(8 + t, 16, stride=Q)
        for c in range(2):
            spread[c, place, :] = spread[c, place, :] + total[:, 128 * c : 128 * c + 128]

    def rg_source(k, chan):
        return spread.at[chan, pl.ds(pl.multiple_of(8 - 8 * half + 16 * k, 8), 16)]

    def rg_copy(k, chan):
        return send(rg_source(k, chan), rg.at[k, half], rg_ss.at[k, chan], rg_rs.at[k, half], k, chan)

    def each_rg(act):
        for k in (4, 3, 2, 1, 0):
            if k == 0:
                act(rg_copy(0, mate))
            else:
                @pl.when(there(k))
                def _(k=k):
                    for chan in range(2):
                        act(rg_copy(k, chan))

    each_rg(lambda c: c.start())
    lg = jnp.concatenate(
        [jnp.sum(g0[v_of(u)].reshape(64, 256), axis=0, keepdims=True) for u in range(8)], axis=0
    )
    low, high = lg[:, :128], lg[:, 128:]
    swap_out[0:8] = jnp.where(half == 0, high, low)
    swap_out[8:16] = contact
    swap_copy = send(swap_out, swap, swap_ss.at[0], swap_rs.at[0], 0, mate)
    swap_copy.start()
    rg[0, half] = spread[half, pl.ds(pl.multiple_of(8 - 8 * half, 8), 16), :]
    mine = pl.ds(pl.multiple_of(8 * half, 8), 8)
    other = pl.ds(pl.multiple_of(8 * mate, 8), 8)
    lg_out[mine, :] = jnp.where(half == 0, low, high)
    contact_out[mine, :] = contact[:, :64]

    for k in range(1, 5):
        @pl.when(jnp.logical_not(there(-k)))
        def _(k=k):
            rg[k] = jnp.zeros(rg.shape[1:], F32)

    swap_copy.wait_recv()
    lg_out[other, :] = swap[0:8]
    contact_out[other, :] = swap[8:16, :64]

    def rg_wait(k, chan):
        send(rg_source(k, chan), rg.at[k, chan], rg_ss.at[k, chan], rg_rs.at[k, chan], 0, mate).wait_recv()

    for k in range(5):
        if k == 0:
            rg_wait(0, mate)
        else:
            @pl.when(there(-k))
            def _(k=k):
                for chan in range(2):
                    rg_wait(k, chan)
    rg_out[...] = sum(rg[k, c] for k in range(5) for c in range(2))

    each_emb(lambda c: c.wait_send())
    for k, a in every_w:
        w_copy(k, a).wait_send()
    ro_copy.wait_send()
    each_cot(lambda c: c.wait_send())
    each_rg(lambda c: c.wait_send())
    swap_copy.wait_send()
    for copies in rims:
        for copy in copies:
            copy.wait_send()


def hand_out(*refs):
    sems = refs[6]
    copies = [pltpu.make_async_copy(refs[n], refs[3 + n], sems.at[n]) for n in range(3)]
    for copy in copies:
        copy.start()
    for copy in copies:
        copy.wait()


def local(slabs, left_embed, right_embed, conv_weight, readout, cotangent):
    vmem = pl.BlockSpec(memory_space=pltpu.VMEM)
    anywhere = pl.BlockSpec(memory_space=pl.ANY)
    dma = pltpu.SemaphoreType.DMA

    def padded(rows, r):
        return pltpu.VMEM((rows, Q + 2 * r, 16, 256), BF16)

    def wide(rows):
        return pltpu.VMEM((rows, Q, 16, 256), F32)

    out_shape = (
        jax.ShapeDtypeStruct((16, 64), F32),
        jax.ShapeDtypeStruct((16, 128), F32),
        jax.ShapeDtypeStruct((16, 128), F32),
    )
    results = pl.pallas_call(
        functools.partial(kernel, slabs),
        out_shape=out_shape,
        in_specs=[vmem, vmem, anywhere, vmem, vmem],
        out_specs=(vmem, vmem, vmem),
        scratch_shapes=[
            pltpu.VMEM((32, 128), BF16),
            pltpu.VMEM((7, 2, 32, 128), BF16),
            pltpu.VMEM((4, 112, 128), F32),
            pltpu.VMEM((2, 3, 3, 3, 256, 128), BF16),
            pltpu.VMEM((48, 128), F32),
            pltpu.VMEM((2, 8, 128), F32),
            padded(24, 1), padded(24, 2), padded(24, 4),
            padded(20, 4), padded(14, 2), padded(11, 1),
            wide(22), wide(20), wide(16), wide(12), wide(10),
            pltpu.VMEM((16, 64, 128), F32), pltpu.VMEM((16, Q, 16, 256), BF16),
            pltpu.VMEM((2, 88, 128), F32),
            pltpu.VMEM((5, 2, 16, 128), F32),
            pltpu.VMEM((16, 128), F32),
            pltpu.VMEM((16, 128), F32),
            dma((7, 2)), dma((7, 2)), dma((3,)), dma((3, 3)), dma((3, 3)),
            dma((2,)), dma((2,)), dma((1,)), dma((1,)),
            dma((5, 2)), dma((5, 2)), dma((1,)), dma((1,)),
            dma((5, 4)), dma((5, 4)),
        ],
        compiler_params=pltpu.CompilerParams(
            collective_id=0, has_side_effects=True, vmem_limit_bytes=56 * 2**20
        ),
        cost_estimate=pl.CostEstimate(flops=8 * 10**9, bytes_accessed=4 * 10**6, transcendentals=10**6),
    )(left_embed, right_embed, conv_weight, readout.reshape(1, 128), cotangent)
    return pl.pallas_call(
        hand_out, out_shape=out_shape, in_specs=[anywhere] * 3, out_specs=(anywhere,) * 3,
        scratch_shapes=[dma((3,))],
    )(*results)


def solution(mesh):
    return jax.shard_map(
        functools.partial(local, mesh.shape["chrom"]),
        mesh=mesh,
        in_specs=(
            P("chrom", "chan"),
            P("chrom", "chan"),
            P(None, None, None, None, "chan"),
            P("chan"),
            P("chrom", None),
        ),
        out_specs=(P("chrom", None), P("chrom", "chan"), P("chrom", "chan")),
        check_vma=False,
    )
```

```python
import functools

import jax
import jax.numpy as jnp
from jax import lax
from jax.experimental import pallas as pl
from jax.experimental.pallas import tpu as pltpu
from jax.sharding import PartitionSpec as P

MESH = pl.DeviceIdType.MESH
F32, BF16 = jnp.float32, jnp.bfloat16
BACK, AHEAD = 1, 5
Q = 4


def split3(x):
    hi = x.astype(BF16)
    rest = x - hi.astype(F32)
    mid = rest.astype(BF16)
    return hi, mid, (rest - mid.astype(F32)).astype(BF16)


def nt(a, b):
    return lax.dot_general(a, b, (((1,), (1,)), ((), ())), preferred_element_type=F32)


def shifted(x, step):
    n = x.shape[2]
    flat = x.reshape((x.shape[0] * x.shape[1],) + x.shape[2:])
    moved = pltpu.roll(flat, step % n, 1)
    where = lax.broadcasted_iota(jnp.int32, flat.shape, 1)
    edge = 0 if step == 1 else n - 1
    return jnp.where(where == edge, 0.0, moved).reshape(x.shape)


def put(buf, row, x, r):
    rows = pl.ds(row, x.shape[0])
    buf[rows, r : r + Q] = x.astype(BF16)
    buf[rows, 0:r] = shifted(x[:, Q - r :], 1).astype(BF16)
    buf[rows, r + Q :] = shifted(x[:, :r], -1).astype(BF16)


def kernel(
    slabs,
    left_ref, right_ref, w_hbm, ro_ref, cot_ref,
    contact_out, lg_out, rg_out,
    block, emb, rwin, w, cot, ro, p0, p1, p2, d2, d1, d0, s0, s1, g2, g1, g0, columns, p3,
    spread, rg, swap_out, swap,
    emb_ss, emb_rs, w_ls, w_ss, w_rs, cot_ss, cot_rs, ro_ss, ro_rs, rg_ss, rg_rs, swap_ss, swap_rs, rim_ss, rim_rs,
):
    slab = lax.axis_index("chrom")
    half = lax.axis_index("chan")
    mate = 1 - half

    def there(delta):
        return jnp.logical_and(slab + delta >= 0, slab + delta < slabs)

    def send(src, dst, ss, rs, delta, chan):
        return pltpu.make_async_remote_copy(
            src_ref=src, dst_ref=dst, send_sem=ss, recv_sem=rs,
            device_id=(slab + delta, chan), device_id_type=MESH,
        )

    sign = 2 * half - 1

    def bin_of(v):
        return 7 + half + sign * v

    barrier = pltpu.get_barrier_semaphore()
    reach = max(BACK, AHEAD)
    for delta in range(-reach, reach + 1):
        if delta == 0:
            pl.semaphore_signal(barrier, inc=1, device_id=(slab, mate), device_id_type=MESH)
        else:
            @pl.when(there(delta))
            def _(delta=delta):
                for chan in range(2):
                    pl.semaphore_signal(barrier, inc=1, device_id=(slab + delta, chan), device_id_type=MESH)

    layers = w.shape[1]
    local = [pltpu.make_async_copy(w_hbm.at[k], w.at[half, k], w_ls.at[k]) for k in range(layers)]
    for copy in local:
        copy.start()
    block[0:16] = right_ref[...]
    block[16:32] = left_ref[...]
    emb[BACK, half] = block[...]
    cot[16:32] = jnp.concatenate([cot_ref[...], jnp.zeros((16, 64), F32)], axis=1)
    ro[half] = jnp.broadcast_to(ro_ref[...], (8, 128))
    for k in range(BACK + AHEAD + 1):
        if k != BACK:
            @pl.when(jnp.logical_not(there(k - BACK)))
            def _(k=k):
                emb[k] = jnp.zeros(emb.shape[1:], BF16)
    for delta in (-1, 1):
        @pl.when(jnp.logical_not(there(delta)))
        def _(delta=delta):
            cot[16 + 16 * delta : 32 + 16 * delta] = jnp.zeros((16, 128), F32)

    pl.semaphore_wait(
        barrier, 2 * (jnp.minimum(slab, reach) + jnp.minimum(slabs - 1 - slab, reach) + 1) - 1
    )

    def emb_copy(delta, chan):
        k = BACK - delta
        return send(block, emb.at[k, half], emb_ss.at[k, chan], emb_rs.at[k, half], delta, chan)

    def each_emb(act):
        for delta in (0, 1, -1, -2, -3, -4, -5):
            if delta == 0:
                act(emb_copy(0, mate))
            else:
                @pl.when(there(delta))
                def _(delta=delta):
                    for chan in range(2):
                        act(emb_copy(delta, chan))

    def w_copy(k, a):
        return send(w_hbm.at[k, a], w.at[half, k, a], w_ss.at[k, a], w_rs.at[k, a], 0, mate)

    every_w = [(k, a) for k in range(layers) for a in range(3)]

    def cot_copy(delta):
        place = pl.ds(16 - 16 * delta, 16)
        slot = (1 - delta) // 2
        return send(cot.at[pl.ds(16, 16)], cot.at[place], cot_ss.at[slot], cot_rs.at[slot], delta, half)

    def each_cot(act):
        for delta in (-1, 1):
            @pl.when(there(delta))
            def _(delta=delta):
                act(cot_copy(delta))

    ro_copy = send(ro.at[half], ro.at[half], ro_ss.at[0], ro_rs.at[0], 0, mate)

    ro_copy.start()
    each_cot(lambda c: c.start())
    each_emb(lambda c: c.start())
    for k, a in every_w:
        w_copy(k, a).start()
    n_i = lax.broadcasted_iota(jnp.int32, (64, 128), 0)
    d_i = lax.broadcasted_iota(jnp.int32, (64, 128), 1)
    order = jnp.where(d_i == Q * (n_i % 16) + n_i // 16, 1.0, 0.0).astype(BF16)

    send(ro.at[half], ro.at[mate], ro_ss.at[0], ro_rs.at[0], 0, mate).wait_recv()
    for delta in (-1, 1):
        @pl.when(there(delta))
        def _(delta=delta):
            slot = (1 + delta) // 2
            send(
                cot.at[pl.ds(16, 16)], cot.at[pl.ds(16 + 16 * delta, 16)],
                cot_ss.at[slot], cot_rs.at[slot], delta, half,
            ).wait_recv()
    readout = jnp.concatenate([ro[0, 0:1], ro[1, 0:1]], axis=1)
    parts = split3(readout)
    row_i = lax.broadcasted_iota(jnp.int32, (16, 256), 0)
    ro_rows = sum(
        jnp.where(row_i == m, jnp.broadcast_to(part.astype(F32), (16, 256)), 0.0) for m, part in enumerate(parts)
    ).astype(BF16)
    cot_win = jnp.concatenate([cot[pl.ds(16 + bin_of(v), 1), :] for v in range(16)], axis=0)
    cot_t = sum(nt(order, part) for part in split3(cot_win))

    for v in range(16):
        columns[v] = jnp.broadcast_to(cot_t[:, v : v + 1], (64, 128))

    def emb_wait(k, chan):
        send(block, emb.at[k, chan], emb_ss.at[k, chan], emb_rs.at[k, chan], 0, mate).wait_recv()

    for k in range(BACK + AHEAD + 1):
        if k == BACK:
            emb_wait(k, mate)
        else:
            @pl.when(there(k - BACK))
            def _(k=k):
                for chan in range(2):
                    emb_wait(k, chan)

    for k in range(BACK + AHEAD + 1):
        for c in range(2):
            rwin[c, 16 * k : 16 * k + 16] = emb[k, c, 0:16].astype(F32)
            if k < 3:
                rwin[2 + c, 16 * k : 16 * k + 16] = emb[k, c, 16:32].astype(F32)

    outer_edge = jnp.logical_or(
        jnp.logical_and(half == 0, slab == 0), jnp.logical_and(half == 1, slab == slabs - 1)
    )

    def clear(buf, r):
        @pl.when(outer_edge)
        def _():
            buf[r + 8 :] = jnp.zeros((buf.shape[0] - r - 8,) + buf.shape[1:], BF16)

    def rim(n, buf, r):
        return [
            send(buf.at[r + j], buf.at[r - 1 - j], rim_ss.at[n, j], rim_rs.at[n, j], 0, mate)
            for j in range(r)
        ]

    rims = [rim(n, buf, r) for n, (buf, r) in enumerate([(p1, 2), (p2, 4), (d2, 4), (d1, 2), (d0, 1)])]

    def rim_start(n):
        for copy in rims[n]:
            copy.start()

    def rim_wait(n):
        for copy in rims[n]:
            copy.wait_recv()

    def first_pair(row, unused):
        place = 16 + bin_of(row - 1)
        left = jnp.concatenate([rwin[2 + c, pl.ds(place, 1), :] for c in range(2)], axis=1)
        tiles = [
            left + jnp.concatenate([rwin[c, pl.ds(place + q, 16, stride=Q), :] for c in range(2)], axis=1)
            for q in range(Q)
        ]
        put(p0, row, jnp.stack(tiles)[None], 1)
        return unused

    lax.fori_loop(0, 24, first_pair, 0)
    clear(p0, 1)

    taps = [2 - 2 * half, 1, 2 * half]

    def weights(k):
        local[k].wait()
        for a in range(3):
            send(w_hbm.at[k, a], w.at[mate, k, a], w_ss.at[k, a], w_rs.at[k, a], 0, mate).wait_recv()

    def forward(k, src, steps, n, sink):
        r = 2**k
        weights(k)

        def step(index, unused):
            begin = index * n
            wide = jnp.concatenate(
                [jnp.concatenate([w[c, k, a].reshape(3 * 256, 128) for a in taps], axis=0) for c in range(2)],
                axis=1,
            )
            lhs = jnp.concatenate(
                [
                    src[pl.ds(begin + m * r, n), b * r : b * r + Q].reshape(n * 64, 256)
                    for m in range(3) for b in range(3)
                ],
                axis=1,
            )
            z = jnp.dot(lhs, wide, preferred_element_type=F32).reshape(n, Q, 16, 256)
            s = 0.5 + 0.5 * jnp.tanh(0.5 * z)
            old = src[pl.ds(begin + r, n), r : r + Q].astype(F32)
            zs = z * s
            sink(index, begin, n, old + zs, s + zs * (1.0 - s))
            return unused

        lax.fori_loop(0, steps, step, 0)

    def rim_after(index, n_rim):
        @pl.when(index == 0)
        def _():
            rim_start(n_rim)

    def keep(buf, r, slopes, n_rim):
        def sink(index, begin, n, x, slope):
            put(buf, begin + r, x, r)
            rim_after(index, n_rim)
            slopes[pl.ds(begin, n)] = slope

        return sink

    forward(0, p0, 2, 11, keep(p1, 2, s0, 0))
    clear(p1, 2)
    each_emb(lambda c: c.wait_send())
    ro_copy.wait_send()
    each_cot(lambda c: c.wait_send())
    rim_wait(0)
    forward(1, p1, 2, 10, keep(p2, 4, s1, 1))
    clear(p2, 4)

    def last_sink(index, begin, n, x, slope):
        column = columns[pl.ds(begin, n)]
        grad = jnp.concatenate([column, column], axis=2) * readout[None]
        grad = grad.reshape(n, Q, 16, 256)
        put(d2, begin + 4, grad * slope, 4)
        rim_after(index, 2)
        g2[pl.ds(begin, n)] = grad
        p3[pl.ds(begin, n)] = x.astype(BF16)

    rim_wait(1)
    forward(2, p2, 2, 8, last_sink)
    clear(d2, 4)
    def backward(k, src, steps, n, before, sink):
        r = 2**k

        def step(index, unused):
            begin = index * n
            wide = jnp.concatenate([w[c, k, a, b] for a in taps for b in range(3) for c in range(2)], axis=1)
            lhs = jnp.concatenate(
                [
                    src[pl.ds(begin + (2 - m) * r, n), (2 - b) * r : (2 - b) * r + Q].reshape(n * 64, 256)
                    for m in range(3) for b in range(3)
                ],
                axis=1,
            )
            sink(index, begin, n, before[pl.ds(begin, n)] + nt(lhs, wide).reshape(n, Q, 16, 256))
            return unused

        lax.fori_loop(0, steps, step, 0)

    def hand_on(buf, r, slopes, grads, n_rim):
        def sink(index, begin, n, grad):
            put(buf, begin + r, grad * slopes[pl.ds(begin, n)], r)
            rim_after(index, n_rim)
            grads[pl.ds(begin, n)] = grad

        return sink

    def last(index, begin, n, grad):
        g0[pl.ds(begin, n)] = grad

    rim_wait(2)
    backward(2, d2, 2, 6, g2, hand_on(d1, 2, s1, g1, 3))
    clear(d1, 2)
    rim_wait(3)
    backward(1, d1, 2, 5, g1, hand_on(d0, 1, s0, g0, 4))
    clear(d0, 1)
    rim_wait(4)
    backward(0, d0, 1, 8, g0, last)

    def v_of(u):
        return (1 - half) * (7 - u) + half * u

    spread[...] = jnp.zeros(spread.shape, F32)
    for t in range(8 + Q - 1):
        total = sum(g0[v_of(t - q), q] for q in range(Q) if 0 <= t - q < 8)
        place = pl.ds(8 + t, 16, stride=Q)
        for c in range(2):
            spread[c, place, :] = spread[c, place, :] + total[:, 128 * c : 128 * c + 128]

    def rg_source(k, chan):
        return spread.at[chan, pl.ds(pl.multiple_of(8 - 8 * half + 16 * k, 8), 16)]

    def rg_copy(k, chan):
        return send(rg_source(k, chan), rg.at[k, half], rg_ss.at[k, chan], rg_rs.at[k, half], k, chan)

    def each_rg(act):
        for k in (4, 3, 2, 1, 0):
            if k == 0:
                act(rg_copy(0, mate))
            else:
                @pl.when(there(k))
                def _(k=k):
                    for chan in range(2):
                        act(rg_copy(k, chan))

    each_rg(lambda c: c.start())
    contacts = [
        jnp.sum(nt(ro_rows, p3[v].reshape(64, 256)), axis=0, keepdims=True) for v in range(8)
    ]
    outwards = jnp.concatenate(contacts, axis=0)
    inwards = jnp.concatenate(contacts[::-1], axis=0)
    contact_rows = jnp.where(half == 1, outwards, inwards)
    contact = sum(jnp.dot(part, order, preferred_element_type=F32) for part in split3(contact_rows))

    lg = jnp.concatenate(
        [jnp.sum(g0[v_of(u)].reshape(64, 256), axis=0, keepdims=True) for u in range(8)], axis=0
    )
    low, high = lg[:, :128], lg[:, 128:]
    swap_out[0:8] = jnp.where(half == 0, high, low)
    swap_out[8:16] = contact
    swap_copy = send(swap_out, swap, swap_ss.at[0], swap_rs.at[0], 0, mate)
    swap_copy.start()
    rg[0, half] = spread[half, pl.ds(pl.multiple_of(8 - 8 * half, 8), 16), :]
    mine = pl.ds(pl.multiple_of(8 * half, 8), 8)
    other = pl.ds(pl.multiple_of(8 * mate, 8), 8)
    lg_out[mine, :] = jnp.where(half == 0, low, high)
    contact_out[mine, :] = contact[:, :64]

    for k in range(1, 5):
        @pl.when(jnp.logical_not(there(-k)))
        def _(k=k):
            rg[k] = jnp.zeros(rg.shape[1:], F32)

    for k, a in every_w:
        w_copy(k, a).wait_send()
    for copies in rims:
        for copy in copies:
            copy.wait_send()
    each_rg(lambda c: c.wait_send())
    swap_copy.wait_send()
    swap_copy.wait_recv()
    lg_out[other, :] = swap[0:8]
    contact_out[other, :] = swap[8:16, :64]

    def rg_wait(k, chan):
        send(rg_source(k, chan), rg.at[k, chan], rg_ss.at[k, chan], rg_rs.at[k, chan], 0, mate).wait_recv()

    for k in range(5):
        if k == 0:
            rg_wait(0, mate)
        else:
            @pl.when(there(-k))
            def _(k=k):
                for chan in range(2):
                    rg_wait(k, chan)
    rg_out[...] = sum(rg[k, c] for k in range(5) for c in range(2))


def hand_out(*refs):
    sems = refs[6]
    copies = [pltpu.make_async_copy(refs[n], refs[3 + n], sems.at[n]) for n in range(3)]
    for copy in copies:
        copy.start()
    for copy in copies:
        copy.wait()


def local(slabs, left_embed, right_embed, conv_weight, readout, cotangent):
    vmem = pl.BlockSpec(memory_space=pltpu.VMEM)
    anywhere = pl.BlockSpec(memory_space=pl.ANY)
    dma = pltpu.SemaphoreType.DMA

    def padded(rows, r):
        return pltpu.VMEM((rows, Q + 2 * r, 16, 256), BF16)

    def wide(rows):
        return pltpu.VMEM((rows, Q, 16, 256), F32)

    out_shape = (
        jax.ShapeDtypeStruct((16, 64), F32),
        jax.ShapeDtypeStruct((16, 128), F32),
        jax.ShapeDtypeStruct((16, 128), F32),
    )
    results = pl.pallas_call(
        functools.partial(kernel, slabs),
        out_shape=out_shape,
        in_specs=[vmem, vmem, anywhere, vmem, vmem],
        out_specs=(vmem, vmem, vmem),
        scratch_shapes=[
            pltpu.VMEM((32, 128), BF16),
            pltpu.VMEM((7, 2, 32, 128), BF16),
            pltpu.VMEM((4, 112, 128), F32),
            pltpu.VMEM((2, 3, 3, 3, 256, 128), BF16),
            pltpu.VMEM((48, 128), F32),
            pltpu.VMEM((2, 8, 128), F32),
            padded(24, 1), padded(24, 2), padded(24, 4),
            padded(20, 4), padded(14, 2), padded(11, 1),
            wide(22), wide(20), wide(16), wide(12), wide(10),
            pltpu.VMEM((16, 64, 128), F32), pltpu.VMEM((16, Q, 16, 256), BF16),
            pltpu.VMEM((2, 88, 128), F32),
            pltpu.VMEM((5, 2, 16, 128), F32),
            pltpu.VMEM((16, 128), F32),
            pltpu.VMEM((16, 128), F32),
            dma((7, 2)), dma((7, 2)), dma((3,)), dma((3, 3)), dma((3, 3)),
            dma((2,)), dma((2,)), dma((1,)), dma((1,)),
            dma((5, 2)), dma((5, 2)), dma((1,)), dma((1,)),
            dma((5, 4)), dma((5, 4)),
        ],
        compiler_params=pltpu.CompilerParams(
            collective_id=0, has_side_effects=True, vmem_limit_bytes=56 * 2**20
        ),
        cost_estimate=pl.CostEstimate(flops=8 * 10**9, bytes_accessed=4 * 10**6, transcendentals=10**6),
    )(left_embed, right_embed, conv_weight, readout.reshape(1, 128), cotangent)
    return pl.pallas_call(
        hand_out, out_shape=out_shape, in_specs=[anywhere] * 3, out_specs=(anywhere,) * 3,
        scratch_shapes=[dma((3,))],
    )(*results)


def solution(mesh):
    return jax.shard_map(
        functools.partial(local, mesh.shape["chrom"]),
        mesh=mesh,
        in_specs=(
            P("chrom", "chan"),
            P("chrom", "chan"),
            P(None, None, None, None, "chan"),
            P("chan"),
            P("chrom", None),
        ),
        out_specs=(P("chrom", None), P("chrom", "chan"), P("chrom", "chan")),
        check_vma=False,
    )
```

```python
import functools

import jax
import jax.numpy as jnp
from jax import lax
from jax.experimental import pallas as pl
from jax.experimental.pallas import tpu as pltpu
from jax.sharding import PartitionSpec as P

MESH = pl.DeviceIdType.MESH
F32, BF16 = jnp.float32, jnp.bfloat16
BACK, AHEAD = 1, 5
Q = 4


def split3(x):
    hi = x.astype(BF16)
    rest = x - hi.astype(F32)
    mid = rest.astype(BF16)
    return hi, mid, (rest - mid.astype(F32)).astype(BF16)


def nt(a, b):
    return lax.dot_general(a, b, (((1,), (1,)), ((), ())), preferred_element_type=F32)


def shifted(x, step):
    n = x.shape[2]
    flat = x.reshape((x.shape[0] * x.shape[1],) + x.shape[2:])
    moved = pltpu.roll(flat, step % n, 1)
    where = lax.broadcasted_iota(jnp.int32, flat.shape, 1)
    edge = 0 if step == 1 else n - 1
    return jnp.where(where == edge, 0.0, moved).reshape(x.shape)


def put(buf, row, x, r):
    rows = pl.ds(row, x.shape[0])
    buf[rows, r : r + Q] = x.astype(BF16)
    buf[rows, 0:r] = shifted(x[:, Q - r :], 1).astype(BF16)
    buf[rows, r + Q :] = shifted(x[:, :r], -1).astype(BF16)


def kernel(
    slabs,
    left_ref, right_ref, w_hbm, ro_ref, cot_ref,
    contact_out, lg_out, rg_out,
    block, emb, rwin, w, cot, ro, p0, p1, p2, d2, d1, d0, s0, s1, g2, g1, g0, columns, p3,
    spread, rg, swap_out, swap,
    emb_ss, emb_rs, w_ls, w_ss, w_rs, cot_ss, cot_rs, ro_ss, ro_rs, rg_ss, rg_rs, swap_ss, swap_rs, rim_ss, rim_rs,
):
    slab = lax.axis_index("chrom")
    half = lax.axis_index("chan")
    mate = 1 - half

    def there(delta):
        return jnp.logical_and(slab + delta >= 0, slab + delta < slabs)

    def send(src, dst, ss, rs, delta, chan):
        return pltpu.make_async_remote_copy(
            src_ref=src, dst_ref=dst, send_sem=ss, recv_sem=rs,
            device_id=(slab + delta, chan), device_id_type=MESH,
        )

    sign = 2 * half - 1

    def bin_of(v):
        return 7 + half + sign * v

    barrier = pltpu.get_barrier_semaphore()
    reach = max(BACK, AHEAD)
    for delta in range(-reach, reach + 1):
        if delta == 0:
            pl.semaphore_signal(barrier, inc=1, device_id=(slab, mate), device_id_type=MESH)
        else:
            @pl.when(there(delta))
            def _(delta=delta):
                for chan in range(2):
                    pl.semaphore_signal(barrier, inc=1, device_id=(slab + delta, chan), device_id_type=MESH)

    layers = w.shape[1]
    local = [pltpu.make_async_copy(w_hbm.at[k], w.at[half, k], w_ls.at[k]) for k in range(layers)]
    for copy in local:
        copy.start()
    block[0:16] = right_ref[...]
    block[16:32] = left_ref[...]
    emb[BACK, half] = block[...]
    cot[16:32] = jnp.concatenate([cot_ref[...], jnp.zeros((16, 64), F32)], axis=1)
    ro[half] = jnp.broadcast_to(ro_ref[...], (8, 128))
    for k in range(BACK + AHEAD + 1):
        if k != BACK:
            @pl.when(jnp.logical_not(there(k - BACK)))
            def _(k=k):
                emb[k] = jnp.zeros(emb.shape[1:], BF16)
    for delta in (-1, 1):
        @pl.when(jnp.logical_not(there(delta)))
        def _(delta=delta):
            cot[16 + 16 * delta : 32 + 16 * delta] = jnp.zeros((16, 128), F32)

    pl.semaphore_wait(
        barrier, 2 * (jnp.minimum(slab, reach) + jnp.minimum(slabs - 1 - slab, reach) + 1) - 1
    )

    def emb_copy(delta, chan):
        k = BACK - delta
        return send(block, emb.at[k, half], emb_ss.at[k, chan], emb_rs.at[k, half], delta, chan)

    def each_emb(act):
        for delta in (0, 1, -1, -2, -3, -4, -5):
            if delta == 0:
                act(emb_copy(0, mate))
            else:
                @pl.when(there(delta))
                def _(delta=delta):
                    for chan in range(2):
                        act(emb_copy(delta, chan))

    distances = {(1, 1): 1, (2, 1): 1, (1, 2): 2, (2, 2): 2, (2, 0): 4} if slabs % 8 == 0 else {}

    def w_copy(k, a):
        far = distances.get((k, a), 0)
        delta = far - 2 * far * (slab // far % 2) if far else 0
        return send(w_hbm.at[k, a], w.at[half, k, a], w_ss.at[k, a], w_rs.at[k, a], delta, mate)

    every_w = [(k, a) for k in range(layers) for a in range(3)]

    def cot_copy(delta):
        place = pl.ds(16 - 16 * delta, 16)
        slot = (1 - delta) // 2
        return send(cot.at[pl.ds(16, 16)], cot.at[place], cot_ss.at[slot], cot_rs.at[slot], delta, half)

    def each_cot(act):
        for delta in (-1, 1):
            @pl.when(there(delta))
            def _(delta=delta):
                act(cot_copy(delta))

    ro_copy = send(ro.at[half], ro.at[half], ro_ss.at[0], ro_rs.at[0], 0, mate)

    ro_copy.start()
    each_cot(lambda c: c.start())
    each_emb(lambda c: c.start())
    for k, a in sorted(every_w, key=lambda piece: distances.get(piece, 0) == 0):
        w_copy(k, a).start()
    n_i = lax.broadcasted_iota(jnp.int32, (64, 128), 0)
    d_i = lax.broadcasted_iota(jnp.int32, (64, 128), 1)
    order = jnp.where(d_i == Q * (n_i % 16) + n_i // 16, 1.0, 0.0).astype(BF16)

    send(ro.at[half], ro.at[mate], ro_ss.at[0], ro_rs.at[0], 0, mate).wait_recv()
    for delta in (-1, 1):
        @pl.when(there(delta))
        def _(delta=delta):
            slot = (1 + delta) // 2
            send(
                cot.at[pl.ds(16, 16)], cot.at[pl.ds(16 + 16 * delta, 16)],
                cot_ss.at[slot], cot_rs.at[slot], delta, half,
            ).wait_recv()
    readout = jnp.concatenate([ro[0, 0:1], ro[1, 0:1]], axis=1)
    parts = split3(readout)
    row_i = lax.broadcasted_iota(jnp.int32, (16, 256), 0)
    ro_rows = sum(
        jnp.where(row_i == m, jnp.broadcast_to(part.astype(F32), (16, 256)), 0.0) for m, part in enumerate(parts)
    ).astype(BF16)
    cot_win = jnp.concatenate([cot[pl.ds(16 + bin_of(v), 1), :] for v in range(16)], axis=0)
    cot_t = sum(nt(order, part) for part in split3(cot_win))

    for v in range(16):
        columns[v] = jnp.broadcast_to(cot_t[:, v : v + 1], (64, 128))

    def emb_wait(k, chan):
        send(block, emb.at[k, chan], emb_ss.at[k, chan], emb_rs.at[k, chan], 0, mate).wait_recv()

    for k in range(BACK + AHEAD + 1):
        if k == BACK:
            emb_wait(k, mate)
        else:
            @pl.when(there(k - BACK))
            def _(k=k):
                for chan in range(2):
                    emb_wait(k, chan)

    for k in range(BACK + AHEAD + 1):
        for c in range(2):
            rwin[c, 16 * k : 16 * k + 16] = emb[k, c, 0:16].astype(F32)
            if k < 3:
                rwin[2 + c, 16 * k : 16 * k + 16] = emb[k, c, 16:32].astype(F32)

    outer_edge = jnp.logical_or(
        jnp.logical_and(half == 0, slab == 0), jnp.logical_and(half == 1, slab == slabs - 1)
    )

    def clear(buf, r):
        @pl.when(outer_edge)
        def _():
            buf[r + 8 :] = jnp.zeros((buf.shape[0] - r - 8,) + buf.shape[1:], BF16)

    def rim(n, buf, r):
        return [
            send(buf.at[r + j], buf.at[r - 1 - j], rim_ss.at[n, j], rim_rs.at[n, j], 0, mate)
            for j in range(r)
        ]

    rims = [rim(n, buf, r) for n, (buf, r) in enumerate([(p1, 2), (p2, 4), (d2, 4), (d1, 2), (d0, 1)])]

    def rim_start(n):
        for copy in rims[n]:
            copy.start()

    def rim_wait(n):
        for copy in rims[n]:
            copy.wait_recv()

    def first_pair(row, unused):
        place = 16 + bin_of(row - 1)
        left = jnp.concatenate([rwin[2 + c, pl.ds(place, 1), :] for c in range(2)], axis=1)
        tiles = [
            left + jnp.concatenate([rwin[c, pl.ds(place + q, 16, stride=Q), :] for c in range(2)], axis=1)
            for q in range(Q)
        ]
        put(p0, row, jnp.stack(tiles)[None], 1)
        return unused

    lax.fori_loop(0, 24, first_pair, 0)
    clear(p0, 1)

    taps = [2 - 2 * half, 1, 2 * half]

    def weights(k):
        local[k].wait()
        for a in range(3):
            send(w_hbm.at[k, a], w.at[mate, k, a], w_ss.at[k, a], w_rs.at[k, a], 0, mate).wait_recv()

    def forward(k, src, steps, n, sink):
        r = 2**k
        weights(k)

        def step(index, unused):
            begin = index * n
            wide = jnp.concatenate(
                [jnp.concatenate([w[c, k, a].reshape(3 * 256, 128) for a in taps], axis=0) for c in range(2)],
                axis=1,
            )
            lhs = jnp.concatenate(
                [
                    src[pl.ds(begin + m * r, n), b * r : b * r + Q].reshape(n * 64, 256)
                    for m in range(3) for b in range(3)
                ],
                axis=1,
            )
            z = jnp.dot(lhs, wide, preferred_element_type=F32).reshape(n, Q, 16, 256)
            s = 0.5 + 0.5 * jnp.tanh(0.5 * z)
            old = src[pl.ds(begin + r, n), r : r + Q].astype(F32)
            zs = z * s
            sink(index, begin, n, old + zs, s + zs * (1.0 - s))
            return unused

        lax.fori_loop(0, steps, step, 0)

    def rim_after(index, n_rim):
        @pl.when(index == 0)
        def _():
            rim_start(n_rim)

    def keep(buf, r, slopes, n_rim):
        def sink(index, begin, n, x, slope):
            put(buf, begin + r, x, r)
            rim_after(index, n_rim)
            slopes[pl.ds(begin, n)] = slope

        return sink

    forward(0, p0, 2, 11, keep(p1, 2, s0, 0))
    clear(p1, 2)
    each_emb(lambda c: c.wait_send())
    ro_copy.wait_send()
    each_cot(lambda c: c.wait_send())
    rim_wait(0)
    forward(1, p1, 2, 10, keep(p2, 4, s1, 1))
    clear(p2, 4)

    def last_sink(index, begin, n, x, slope):
        column = columns[pl.ds(begin, n)]
        grad = jnp.concatenate([column, column], axis=2) * readout[None]
        grad = grad.reshape(n, Q, 16, 256)
        put(d2, begin + 4, grad * slope, 4)
        rim_after(index, 2)
        g2[pl.ds(begin, n)] = grad
        p3[pl.ds(begin, n)] = x.astype(BF16)

    rim_wait(1)
    forward(2, p2, 2, 8, last_sink)
    clear(d2, 4)
    def backward(k, src, steps, n, before, sink):
        r = 2**k

        def step(index, unused):
            begin = index * n
            wide = jnp.concatenate([w[c, k, a, b] for a in taps for b in range(3) for c in range(2)], axis=1)
            lhs = jnp.concatenate(
                [
                    src[pl.ds(begin + (2 - m) * r, n), (2 - b) * r : (2 - b) * r + Q].reshape(n * 64, 256)
                    for m in range(3) for b in range(3)
                ],
                axis=1,
            )
            sink(index, begin, n, before[pl.ds(begin, n)] + nt(lhs, wide).reshape(n, Q, 16, 256))
            return unused

        lax.fori_loop(0, steps, step, 0)

    def hand_on(buf, r, slopes, grads, n_rim):
        def sink(index, begin, n, grad):
            put(buf, begin + r, grad * slopes[pl.ds(begin, n)], r)
            rim_after(index, n_rim)
            grads[pl.ds(begin, n)] = grad

        return sink

    def last(index, begin, n, grad):
        g0[pl.ds(begin, n)] = grad

    rim_wait(2)
    backward(2, d2, 2, 6, g2, hand_on(d1, 2, s1, g1, 3))
    clear(d1, 2)
    rim_wait(3)
    backward(1, d1, 2, 5, g1, hand_on(d0, 1, s0, g0, 4))
    clear(d0, 1)
    rim_wait(4)
    backward(0, d0, 1, 8, g0, last)

    def v_of(u):
        return (1 - half) * (7 - u) + half * u

    spread[...] = jnp.zeros(spread.shape, F32)
    for t in range(8 + Q - 1):
        total = sum(g0[v_of(t - q), q] for q in range(Q) if 0 <= t - q < 8)
        place = pl.ds(8 + t, 16, stride=Q)
        for c in range(2):
            spread[c, place, :] = spread[c, place, :] + total[:, 128 * c : 128 * c + 128]

    def rg_source(k, chan):
        return spread.at[chan, pl.ds(pl.multiple_of(8 - 8 * half + 16 * k, 8), 16)]

    def rg_copy(k, chan):
        return send(rg_source(k, chan), rg.at[k, half], rg_ss.at[k, chan], rg_rs.at[k, half], k, chan)

    def each_rg(act):
        for k in (4, 3, 2, 1, 0):
            if k == 0:
                act(rg_copy(0, mate))
            else:
                @pl.when(there(k))
                def _(k=k):
                    for chan in range(2):
                        act(rg_copy(k, chan))

    each_rg(lambda c: c.start())
    contacts = [
        jnp.sum(nt(ro_rows, p3[v].reshape(64, 256)), axis=0, keepdims=True) for v in range(8)
    ]
    outwards = jnp.concatenate(contacts, axis=0)
    inwards = jnp.concatenate(contacts[::-1], axis=0)
    contact_rows = jnp.where(half == 1, outwards, inwards)
    contact = sum(jnp.dot(part, order, preferred_element_type=F32) for part in split3(contact_rows))

    lg = jnp.concatenate(
        [jnp.sum(g0[v_of(u)].reshape(64, 256), axis=0, keepdims=True) for u in range(8)], axis=0
    )
    low, high = lg[:, :128], lg[:, 128:]
    swap_out[0:8] = jnp.where(half == 0, high, low)
    swap_out[8:16] = contact
    swap_copy = send(swap_out, swap, swap_ss.at[0], swap_rs.at[0], 0, mate)
    swap_copy.start()
    rg[0, half] = spread[half, pl.ds(pl.multiple_of(8 - 8 * half, 8), 16), :]
    mine = pl.ds(pl.multiple_of(8 * half, 8), 8)
    other = pl.ds(pl.multiple_of(8 * mate, 8), 8)
    lg_out[mine, :] = jnp.where(half == 0, low, high)
    contact_out[mine, :] = contact[:, :64]

    for k in range(1, 5):
        @pl.when(jnp.logical_not(there(-k)))
        def _(k=k):
            rg[k] = jnp.zeros(rg.shape[1:], F32)

    for k, a in every_w:
        w_copy(k, a).wait_send()
    for copies in rims:
        for copy in copies:
            copy.wait_send()
    each_rg(lambda c: c.wait_send())
    swap_copy.wait_send()
    swap_copy.wait_recv()
    lg_out[other, :] = swap[0:8]
    contact_out[other, :] = swap[8:16, :64]

    def rg_wait(k, chan):
        send(rg_source(k, chan), rg.at[k, chan], rg_ss.at[k, chan], rg_rs.at[k, chan], 0, mate).wait_recv()

    for k in range(5):
        if k == 0:
            rg_wait(0, mate)
        else:
            @pl.when(there(-k))
            def _(k=k):
                for chan in range(2):
                    rg_wait(k, chan)
    rg_out[...] = sum(rg[k, c] for k in range(5) for c in range(2))


def hand_out(*refs):
    sems = refs[6]
    copies = [pltpu.make_async_copy(refs[n], refs[3 + n], sems.at[n]) for n in range(3)]
    for copy in copies:
        copy.start()
    for copy in copies:
        copy.wait()


def local(slabs, left_embed, right_embed, conv_weight, readout, cotangent):
    vmem = pl.BlockSpec(memory_space=pltpu.VMEM)
    anywhere = pl.BlockSpec(memory_space=pl.ANY)
    dma = pltpu.SemaphoreType.DMA

    def padded(rows, r):
        return pltpu.VMEM((rows, Q + 2 * r, 16, 256), BF16)

    def wide(rows):
        return pltpu.VMEM((rows, Q, 16, 256), F32)

    out_shape = (
        jax.ShapeDtypeStruct((16, 64), F32),
        jax.ShapeDtypeStruct((16, 128), F32),
        jax.ShapeDtypeStruct((16, 128), F32),
    )
    results = pl.pallas_call(
        functools.partial(kernel, slabs),
        out_shape=out_shape,
        in_specs=[vmem, vmem, anywhere, vmem, vmem],
        out_specs=(vmem, vmem, vmem),
        scratch_shapes=[
            pltpu.VMEM((32, 128), BF16),
            pltpu.VMEM((7, 2, 32, 128), BF16),
            pltpu.VMEM((4, 112, 128), F32),
            pltpu.VMEM((2, 3, 3, 3, 256, 128), BF16),
            pltpu.VMEM((48, 128), F32),
            pltpu.VMEM((2, 8, 128), F32),
            padded(24, 1), padded(24, 2), padded(24, 4),
            padded(20, 4), padded(14, 2), padded(11, 1),
            wide(22), wide(20), wide(16), wide(12), wide(10),
            pltpu.VMEM((16, 64, 128), F32), pltpu.VMEM((16, Q, 16, 256), BF16),
            pltpu.VMEM((2, 88, 128), F32),
            pltpu.VMEM((5, 2, 16, 128), F32),
            pltpu.VMEM((16, 128), F32),
            pltpu.VMEM((16, 128), F32),
            dma((7, 2)), dma((7, 2)), dma((3,)), dma((3, 3)), dma((3, 3)),
            dma((2,)), dma((2,)), dma((1,)), dma((1,)),
            dma((5, 2)), dma((5, 2)), dma((1,)), dma((1,)),
            dma((5, 4)), dma((5, 4)),
        ],
        compiler_params=pltpu.CompilerParams(
            collective_id=0, has_side_effects=True, vmem_limit_bytes=56 * 2**20
        ),
        cost_estimate=pl.CostEstimate(flops=8 * 10**9, bytes_accessed=4 * 10**6, transcendentals=10**6),
    )(left_embed, right_embed, conv_weight, readout.reshape(1, 128), cotangent)
    return pl.pallas_call(
        hand_out, out_shape=out_shape, in_specs=[anywhere] * 3, out_specs=(anywhere,) * 3,
        scratch_shapes=[dma((3,))],
    )(*results)


def solution(mesh):
    return jax.shard_map(
        functools.partial(local, mesh.shape["chrom"]),
        mesh=mesh,
        in_specs=(
            P("chrom", "chan"),
            P("chrom", "chan"),
            P(None, None, None, None, "chan"),
            P("chan"),
            P("chrom", None),
        ),
        out_specs=(P("chrom", None), P("chrom", "chan"), P("chrom", "chan")),
        check_vma=False,
    )
```

```python
import functools

import jax
import jax.numpy as jnp
from jax import lax
from jax.experimental import pallas as pl
from jax.experimental.pallas import tpu as pltpu
from jax.sharding import PartitionSpec as P

MESH = pl.DeviceIdType.MESH
F32, BF16 = jnp.float32, jnp.bfloat16
BACK, AHEAD = 1, 5
Q = 4


def split3(x):
    hi = x.astype(BF16)
    rest = x - hi.astype(F32)
    mid = rest.astype(BF16)
    return hi, mid, (rest - mid.astype(F32)).astype(BF16)


def nt(a, b):
    return lax.dot_general(a, b, (((1,), (1,)), ((), ())), preferred_element_type=F32)


def shifted(x, step):
    n = x.shape[2]
    flat = x.reshape((x.shape[0] * x.shape[1],) + x.shape[2:])
    moved = pltpu.roll(flat, step % n, 1)
    where = lax.broadcasted_iota(jnp.int32, flat.shape, 1)
    edge = 0 if step == 1 else n - 1
    return jnp.where(where == edge, 0.0, moved).reshape(x.shape)


def put(buf, row, x, r):
    rows = pl.ds(row, x.shape[0])
    buf[rows, r : r + Q] = x.astype(BF16)
    buf[rows, 0:r] = shifted(x[:, Q - r :], 1).astype(BF16)
    buf[rows, r + Q :] = shifted(x[:, :r], -1).astype(BF16)


def kernel(
    slabs,
    left_ref, right_ref, w_hbm, ro_ref, cot_ref,
    contact_out, lg_out, rg_out,
    block, emb, rwin, w, wt, cot, ro, p0, p1, p2, d2, d1, d0, s0, s1, g2, g1, g0, columns, p3,
    spread, rg, swap_out, swap,
    emb_ss, emb_rs, w_ls, w_ss, w_rs, cot_ss, cot_rs, ro_ss, ro_rs, rg_ss, rg_rs, swap_ss, swap_rs, rim_ss, rim_rs,
):
    slab = lax.axis_index("chrom")
    half = lax.axis_index("chan")
    mate = 1 - half

    def there(delta):
        return jnp.logical_and(slab + delta >= 0, slab + delta < slabs)

    def send(src, dst, ss, rs, delta, chan):
        return pltpu.make_async_remote_copy(
            src_ref=src, dst_ref=dst, send_sem=ss, recv_sem=rs,
            device_id=(slab + delta, chan), device_id_type=MESH,
        )

    sign = 2 * half - 1

    def bin_of(v):
        return 7 + half + sign * v

    barrier = pltpu.get_barrier_semaphore()
    reach = max(BACK, AHEAD)
    for delta in range(-reach, reach + 1):
        if delta == 0:
            pl.semaphore_signal(barrier, inc=1, device_id=(slab, mate), device_id_type=MESH)
        else:
            @pl.when(there(delta))
            def _(delta=delta):
                for chan in range(2):
                    pl.semaphore_signal(barrier, inc=1, device_id=(slab + delta, chan), device_id_type=MESH)

    layers = w.shape[1]
    local = [pltpu.make_async_copy(w_hbm.at[k], w.at[half, k], w_ls.at[k]) for k in range(layers)]
    for copy in local:
        copy.start()
    block[0:16] = right_ref[...]
    block[16:32] = left_ref[...]
    emb[BACK, half] = block[...]
    cot[16:32] = jnp.concatenate([cot_ref[...], jnp.zeros((16, 64), F32)], axis=1)
    ro[half] = jnp.broadcast_to(ro_ref[...], (8, 128))
    for k in range(BACK + AHEAD + 1):
        if k != BACK:
            @pl.when(jnp.logical_not(there(k - BACK)))
            def _(k=k):
                emb[k] = jnp.zeros(emb.shape[1:], BF16)
    for delta in (-1, 1):
        @pl.when(jnp.logical_not(there(delta)))
        def _(delta=delta):
            cot[16 + 16 * delta : 32 + 16 * delta] = jnp.zeros((16, 128), F32)

    pl.semaphore_wait(
        barrier, 2 * (jnp.minimum(slab, reach) + jnp.minimum(slabs - 1 - slab, reach) + 1) - 1
    )

    def emb_copy(delta, chan):
        k = BACK - delta
        return send(block, emb.at[k, half], emb_ss.at[k, chan], emb_rs.at[k, half], delta, chan)

    def each_emb(act):
        for delta in (0, 1, -1, -2, -3, -4, -5):
            if delta == 0:
                act(emb_copy(0, mate))
            else:
                @pl.when(there(delta))
                def _(delta=delta):
                    for chan in range(2):
                        act(emb_copy(delta, chan))

    def w_copy(k, a):
        return send(w_hbm.at[k, a], w.at[half, k, a], w_ss.at[k, a], w_rs.at[k, a], 0, mate)

    every_w = [(k, a) for k in range(layers) for a in range(3)]

    def cot_copy(delta):
        place = pl.ds(16 - 16 * delta, 16)
        slot = (1 - delta) // 2
        return send(cot.at[pl.ds(16, 16)], cot.at[place], cot_ss.at[slot], cot_rs.at[slot], delta, half)

    def each_cot(act):
        for delta in (-1, 1):
            @pl.when(there(delta))
            def _(delta=delta):
                act(cot_copy(delta))

    ro_copy = send(ro.at[half], ro.at[half], ro_ss.at[0], ro_rs.at[0], 0, mate)

    ro_copy.start()
    each_cot(lambda c: c.start())
    each_emb(lambda c: c.start())
    for k, a in every_w:
        w_copy(k, a).start()
    n_i = lax.broadcasted_iota(jnp.int32, (64, 128), 0)
    d_i = lax.broadcasted_iota(jnp.int32, (64, 128), 1)
    order = jnp.where(d_i == Q * (n_i % 16) + n_i // 16, 1.0, 0.0).astype(BF16)

    send(ro.at[half], ro.at[mate], ro_ss.at[0], ro_rs.at[0], 0, mate).wait_recv()
    for delta in (-1, 1):
        @pl.when(there(delta))
        def _(delta=delta):
            slot = (1 + delta) // 2
            send(
                cot.at[pl.ds(16, 16)], cot.at[pl.ds(16 + 16 * delta, 16)],
                cot_ss.at[slot], cot_rs.at[slot], delta, half,
            ).wait_recv()
    readout = jnp.concatenate([ro[0, 0:1], ro[1, 0:1]], axis=1)
    parts = split3(readout)
    row_i = lax.broadcasted_iota(jnp.int32, (16, 256), 0)
    ro_rows = sum(
        jnp.where(row_i == m, jnp.broadcast_to(part.astype(F32), (16, 256)), 0.0) for m, part in enumerate(parts)
    ).astype(BF16)
    cot_win = jnp.concatenate([cot[pl.ds(16 + bin_of(v), 1), :] for v in range(16)], axis=0)
    cot_t = sum(nt(order, part) for part in split3(cot_win))

    for v in range(16):
        columns[v] = jnp.broadcast_to(cot_t[:, v : v + 1], (64, 128))

    def turn(k, chan):
        def one(tap, unused):
            wt[chan, k, tap // 3, tap % 3] = w[chan, k, tap // 3, tap % 3].T
            return unused

        lax.fori_loop(0, 9, one, 0)

    for k in range(layers):
        local[k].wait()
        turn(k, half)

    def emb_wait(k, chan):
        send(block, emb.at[k, chan], emb_ss.at[k, chan], emb_rs.at[k, chan], 0, mate).wait_recv()

    for k in range(BACK + AHEAD + 1):
        if k == BACK:
            emb_wait(k, mate)
        else:
            @pl.when(there(k - BACK))
            def _(k=k):
                for chan in range(2):
                    emb_wait(k, chan)

    for k in range(BACK + AHEAD + 1):
        for c in range(2):
            rwin[c, 16 * k : 16 * k + 16] = emb[k, c, 0:16].astype(F32)
            if k < 3:
                rwin[2 + c, 16 * k : 16 * k + 16] = emb[k, c, 16:32].astype(F32)

    outer_edge = jnp.logical_or(
        jnp.logical_and(half == 0, slab == 0), jnp.logical_and(half == 1, slab == slabs - 1)
    )

    def clear(buf, r):
        @pl.when(outer_edge)
        def _():
            buf[r + 8 :] = jnp.zeros((buf.shape[0] - r - 8,) + buf.shape[1:], BF16)

    def rim(n, buf, r):
        return [
            send(buf.at[r + j], buf.at[r - 1 - j], rim_ss.at[n, j], rim_rs.at[n, j], 0, mate)
            for j in range(r)
        ]

    rims = [rim(n, buf, r) for n, (buf, r) in enumerate([(p1, 2), (p2, 4), (d2, 4), (d1, 2), (d0, 1)])]

    def rim_start(n):
        for copy in rims[n]:
            copy.start()

    def rim_wait(n):
        for copy in rims[n]:
            copy.wait_recv()

    def first_pair(row, unused):
        place = 16 + bin_of(row - 1)
        left = jnp.concatenate([rwin[2 + c, pl.ds(place, 1), :] for c in range(2)], axis=1)
        tiles = [
            left + jnp.concatenate([rwin[c, pl.ds(place + q, 16, stride=Q), :] for c in range(2)], axis=1)
            for q in range(Q)
        ]
        put(p0, row, jnp.stack(tiles)[None], 1)
        return unused

    lax.fori_loop(0, 24, first_pair, 0)
    clear(p0, 1)

    taps = [2 - 2 * half, 1, 2 * half]

    def weights(k):
        for a in range(3):
            send(w_hbm.at[k, a], w.at[mate, k, a], w_ss.at[k, a], w_rs.at[k, a], 0, mate).wait_recv()

    def forward(k, src, steps, n, sink):
        r = 2**k
        weights(k)

        def step(index, unused):
            begin = index * n
            wide = jnp.concatenate(
                [jnp.concatenate([w[c, k, a].reshape(3 * 256, 128) for a in taps], axis=0) for c in range(2)],
                axis=1,
            )
            lhs = jnp.concatenate(
                [
                    src[pl.ds(begin + m * r, n), b * r : b * r + Q].reshape(n * 64, 256)
                    for m in range(3) for b in range(3)
                ],
                axis=1,
            )
            z = jnp.dot(lhs, wide, preferred_element_type=F32).reshape(n, Q, 16, 256)
            s = 0.5 + 0.5 * jnp.tanh(0.5 * z)
            old = src[pl.ds(begin + r, n), r : r + Q].astype(F32)
            zs = z * s
            sink(index, begin, n, old + zs, s + zs * (1.0 - s))
            return unused

        lax.fori_loop(0, steps, step, 0)

    def rim_after(index, n_rim):
        @pl.when(index == 0)
        def _():
            rim_start(n_rim)

    def keep(buf, r, slopes, n_rim):
        def sink(index, begin, n, x, slope):
            put(buf, begin + r, x, r)
            rim_after(index, n_rim)
            slopes[pl.ds(begin, n)] = slope

        return sink

    forward(0, p0, 2, 11, keep(p1, 2, s0, 0))
    clear(p1, 2)
    each_emb(lambda c: c.wait_send())
    ro_copy.wait_send()
    each_cot(lambda c: c.wait_send())
    turn(0, mate)
    rim_wait(0)
    forward(1, p1, 2, 10, keep(p2, 4, s1, 1))
    clear(p2, 4)

    def last_sink(index, begin, n, x, slope):
        column = columns[pl.ds(begin, n)]
        grad = jnp.concatenate([column, column], axis=2) * readout[None]
        grad = grad.reshape(n, Q, 16, 256)
        put(d2, begin + 4, grad * slope, 4)
        rim_after(index, 2)
        g2[pl.ds(begin, n)] = grad
        p3[pl.ds(begin, n)] = x.astype(BF16)

    turn(1, mate)
    rim_wait(1)
    forward(2, p2, 2, 8, last_sink)
    clear(d2, 4)
    def backward(k, src, steps, n, before, sink):
        r = 2**k

        def step(index, unused):
            begin = index * n
            wide = jnp.concatenate([wt[c, k, a, b] for a in taps for b in range(3) for c in range(2)], axis=0)
            lhs = jnp.concatenate(
                [
                    src[pl.ds(begin + (2 - m) * r, n), (2 - b) * r : (2 - b) * r + Q].reshape(n * 64, 256)
                    for m in range(3) for b in range(3)
                ],
                axis=1,
            )
            sink(index, begin, n, before[pl.ds(begin, n)]
                 + jnp.dot(lhs, wide, preferred_element_type=F32).reshape(n, Q, 16, 256))
            return unused

        lax.fori_loop(0, steps, step, 0)

    def hand_on(buf, r, slopes, grads, n_rim):
        def sink(index, begin, n, grad):
            put(buf, begin + r, grad * slopes[pl.ds(begin, n)], r)
            rim_after(index, n_rim)
            grads[pl.ds(begin, n)] = grad

        return sink

    def last(index, begin, n, grad):
        g0[pl.ds(begin, n)] = grad

    turn(2, mate)
    rim_wait(2)
    backward(2, d2, 2, 6, g2, hand_on(d1, 2, s1, g1, 3))
    clear(d1, 2)
    rim_wait(3)
    backward(1, d1, 2, 5, g1, hand_on(d0, 1, s0, g0, 4))
    clear(d0, 1)
    rim_wait(4)
    backward(0, d0, 1, 8, g0, last)

    def v_of(u):
        return (1 - half) * (7 - u) + half * u

    spread[...] = jnp.zeros(spread.shape, F32)
    for t in range(8 + Q - 1):
        total = sum(g0[v_of(t - q), q] for q in range(Q) if 0 <= t - q < 8)
        place = pl.ds(8 + t, 16, stride=Q)
        for c in range(2):
            spread[c, place, :] = spread[c, place, :] + total[:, 128 * c : 128 * c + 128]

    def rg_source(k, chan):
        return spread.at[chan, pl.ds(pl.multiple_of(8 - 8 * half + 16 * k, 8), 16)]

    def rg_copy(k, chan):
        return send(rg_source(k, chan), rg.at[k, half], rg_ss.at[k, chan], rg_rs.at[k, half], k, chan)

    def each_rg(act):
        for k in (4, 3, 2, 1, 0):
            if k == 0:
                act(rg_copy(0, mate))
            else:
                @pl.when(there(k))
                def _(k=k):
                    for chan in range(2):
                        act(rg_copy(k, chan))

    each_rg(lambda c: c.start())
    contacts = [
        jnp.sum(nt(ro_rows, p3[v].reshape(64, 256)), axis=0, keepdims=True) for v in range(8)
    ]
    outwards = jnp.concatenate(contacts, axis=0)
    inwards = jnp.concatenate(contacts[::-1], axis=0)
    contact_rows = jnp.where(half == 1, outwards, inwards)
    contact = sum(jnp.dot(part, order, preferred_element_type=F32) for part in split3(contact_rows))

    lg = jnp.concatenate(
        [jnp.sum(g0[v_of(u)].reshape(64, 256), axis=0, keepdims=True) for u in range(8)], axis=0
    )
    low, high = lg[:, :128], lg[:, 128:]
    swap_out[0:8] = jnp.where(half == 0, high, low)
    swap_out[8:16] = contact
    swap_copy = send(swap_out, swap, swap_ss.at[0], swap_rs.at[0], 0, mate)
    swap_copy.start()
    rg[0, half] = spread[half, pl.ds(pl.multiple_of(8 - 8 * half, 8), 16), :]
    mine = pl.ds(pl.multiple_of(8 * half, 8), 8)
    other = pl.ds(pl.multiple_of(8 * mate, 8), 8)
    lg_out[mine, :] = jnp.where(half == 0, low, high)
    contact_out[mine, :] = contact[:, :64]

    for k in range(1, 5):
        @pl.when(jnp.logical_not(there(-k)))
        def _(k=k):
            rg[k] = jnp.zeros(rg.shape[1:], F32)

    for k, a in every_w:
        w_copy(k, a).wait_send()
    for copies in rims:
        for copy in copies:
            copy.wait_send()
    each_rg(lambda c: c.wait_send())
    swap_copy.wait_send()
    swap_copy.wait_recv()
    lg_out[other, :] = swap[0:8]
    contact_out[other, :] = swap[8:16, :64]

    def rg_wait(k, chan):
        send(rg_source(k, chan), rg.at[k, chan], rg_ss.at[k, chan], rg_rs.at[k, chan], 0, mate).wait_recv()

    for k in range(5):
        if k == 0:
            rg_wait(0, mate)
        else:
            @pl.when(there(-k))
            def _(k=k):
                for chan in range(2):
                    rg_wait(k, chan)
    rg_out[...] = sum(rg[k, c] for k in range(5) for c in range(2))


def hand_out(*refs):
    sems = refs[6]
    copies = [pltpu.make_async_copy(refs[n], refs[3 + n], sems.at[n]) for n in range(3)]
    for copy in copies:
        copy.start()
    for copy in copies:
        copy.wait()


def local(slabs, left_embed, right_embed, conv_weight, readout, cotangent):
    vmem = pl.BlockSpec(memory_space=pltpu.VMEM)
    anywhere = pl.BlockSpec(memory_space=pl.ANY)
    dma = pltpu.SemaphoreType.DMA

    def padded(rows, r):
        return pltpu.VMEM((rows, Q + 2 * r, 16, 256), BF16)

    def wide(rows):
        return pltpu.VMEM((rows, Q, 16, 256), F32)

    out_shape = (
        jax.ShapeDtypeStruct((16, 64), F32),
        jax.ShapeDtypeStruct((16, 128), F32),
        jax.ShapeDtypeStruct((16, 128), F32),
    )
    results = pl.pallas_call(
        functools.partial(kernel, slabs),
        out_shape=out_shape,
        in_specs=[vmem, vmem, anywhere, vmem, vmem],
        out_specs=(vmem, vmem, vmem),
        scratch_shapes=[
            pltpu.VMEM((32, 128), BF16),
            pltpu.VMEM((7, 2, 32, 128), BF16),
            pltpu.VMEM((4, 112, 128), F32),
            pltpu.VMEM((2, 3, 3, 3, 256, 128), BF16),
            pltpu.VMEM((2, 3, 3, 3, 128, 256), BF16),
            pltpu.VMEM((48, 128), F32),
            pltpu.VMEM((2, 8, 128), F32),
            padded(24, 1), padded(24, 2), padded(24, 4),
            padded(20, 4), padded(14, 2), padded(11, 1),
            wide(22), wide(20), wide(16), wide(12), wide(10),
            pltpu.VMEM((16, 64, 128), F32), pltpu.VMEM((16, Q, 16, 256), BF16),
            pltpu.VMEM((2, 88, 128), F32),
            pltpu.VMEM((5, 2, 16, 128), F32),
            pltpu.VMEM((16, 128), F32),
            pltpu.VMEM((16, 128), F32),
            dma((7, 2)), dma((7, 2)), dma((3,)), dma((3, 3)), dma((3, 3)),
            dma((2,)), dma((2,)), dma((1,)), dma((1,)),
            dma((5, 2)), dma((5, 2)), dma((1,)), dma((1,)),
            dma((5, 4)), dma((5, 4)),
        ],
        compiler_params=pltpu.CompilerParams(
            collective_id=0, has_side_effects=True, vmem_limit_bytes=56 * 2**20
        ),
        cost_estimate=pl.CostEstimate(flops=8 * 10**9, bytes_accessed=4 * 10**6, transcendentals=10**6),
    )(left_embed, right_embed, conv_weight, readout.reshape(1, 128), cotangent)
    return pl.pallas_call(
        hand_out, out_shape=out_shape, in_specs=[anywhere] * 3, out_specs=(anywhere,) * 3,
        scratch_shapes=[dma((3,))],
    )(*results)


def solution(mesh):
    return jax.shard_map(
        functools.partial(local, mesh.shape["chrom"]),
        mesh=mesh,
        in_specs=(
            P("chrom", "chan"),
            P("chrom", "chan"),
            P(None, None, None, None, "chan"),
            P("chan"),
            P("chrom", None),
        ),
        out_specs=(P("chrom", None), P("chrom", "chan"), P("chrom", "chan")),
        check_vma=False,
    )
```

```python
import functools

import jax
import jax.numpy as jnp
from jax import lax
from jax.experimental import pallas as pl
from jax.experimental.pallas import tpu as pltpu
from jax.sharding import PartitionSpec as P

MESH = pl.DeviceIdType.MESH
F32, BF16 = jnp.float32, jnp.bfloat16
BACK, AHEAD = 1, 5
Q = 4


def split3(x):
    hi = x.astype(BF16)
    rest = x - hi.astype(F32)
    mid = rest.astype(BF16)
    return hi, mid, (rest - mid.astype(F32)).astype(BF16)


def nt(a, b):
    return lax.dot_general(a, b, (((1,), (1,)), ((), ())), preferred_element_type=F32)


def shifted(x, step):
    n = x.shape[2]
    flat = x.reshape((x.shape[0] * x.shape[1],) + x.shape[2:])
    moved = pltpu.roll(flat, step % n, 1)
    where = lax.broadcasted_iota(jnp.int32, flat.shape, 1)
    edge = 0 if step == 1 else n - 1
    return jnp.where(where == edge, 0.0, moved).reshape(x.shape)


def put(buf, row, x, r):
    rows = pl.ds(row, x.shape[0])
    buf[rows, r : r + Q] = x.astype(BF16)
    buf[rows, 0:r] = shifted(x[:, Q - r :], 1).astype(BF16)
    buf[rows, r + Q :] = shifted(x[:, :r], -1).astype(BF16)


def kernel(
    slabs,
    left_ref, right_ref, w_hbm, ro_ref, cot_ref,
    contact_out, lg_out, rg_out,
    block, emb, rwin, w, cot, ro, p0, p1, p2, d2, d1, d0, s0, s1, g2, g1, g0, columns, p3,
    spread, rg, swap_out, swap,
    emb_ss, emb_rs, w_ls, w_ss, w_rs, cot_ss, cot_rs, ro_ss, ro_rs, rg_ss, rg_rs, swap_ss, swap_rs, rim_ss, rim_rs,
):
    slab = lax.axis_index("chrom")
    half = lax.axis_index("chan")
    mate = 1 - half

    def there(delta):
        return jnp.logical_and(slab + delta >= 0, slab + delta < slabs)

    def send(src, dst, ss, rs, delta, chan):
        return pltpu.make_async_remote_copy(
            src_ref=src, dst_ref=dst, send_sem=ss, recv_sem=rs,
            device_id=(slab + delta, chan), device_id_type=MESH,
        )

    sign = 2 * half - 1

    def bin_of(v):
        return 7 + half + sign * v

    barrier = pltpu.get_barrier_semaphore()
    reach = max(BACK, AHEAD)
    for delta in range(-reach, reach + 1):
        if delta == 0:
            pl.semaphore_signal(barrier, inc=1, device_id=(slab, mate), device_id_type=MESH)
        else:
            @pl.when(there(delta))
            def _(delta=delta):
                for chan in range(2):
                    pl.semaphore_signal(barrier, inc=1, device_id=(slab + delta, chan), device_id_type=MESH)

    layers = w.shape[1]
    local = [pltpu.make_async_copy(w_hbm.at[k], w.at[half, k], w_ls.at[k]) for k in range(layers)]
    for copy in local:
        copy.start()
    block[0:16] = right_ref[...]
    block[16:32] = left_ref[...]
    emb[BACK, half] = block[...]
    cot[16:32] = jnp.concatenate([cot_ref[...], jnp.zeros((16, 64), F32)], axis=1)
    ro[half] = jnp.broadcast_to(ro_ref[...], (8, 128))
    for k in range(BACK + AHEAD + 1):
        if k != BACK:
            @pl.when(jnp.logical_not(there(k - BACK)))
            def _(k=k):
                emb[k] = jnp.zeros(emb.shape[1:], BF16)
    for delta in (-1, 1):
        @pl.when(jnp.logical_not(there(delta)))
        def _(delta=delta):
            cot[16 + 16 * delta : 32 + 16 * delta] = jnp.zeros((16, 128), F32)

    pl.semaphore_wait(
        barrier, 2 * (jnp.minimum(slab, reach) + jnp.minimum(slabs - 1 - slab, reach) + 1) - 1
    )

    def emb_copy(delta, chan):
        k = BACK - delta
        return send(block, emb.at[k, half], emb_ss.at[k, chan], emb_rs.at[k, half], delta, chan)

    def each_emb(act):
        for delta in (0, 1, -1, -2, -3, -4, -5):
            if delta == 0:
                act(emb_copy(0, mate))
            else:
                @pl.when(there(delta))
                def _(delta=delta):
                    for chan in range(2):
                        act(emb_copy(delta, chan))

    def w_copy(k, a):
        return send(w_hbm.at[k, a], w.at[half, k, a], w_ss.at[k, a], w_rs.at[k, a], 0, mate)

    every_w = [(k, a) for k in range(layers) for a in range(3)]

    def cot_copy(delta):
        place = pl.ds(16 - 16 * delta, 16)
        slot = (1 - delta) // 2
        return send(cot.at[pl.ds(16, 16)], cot.at[place], cot_ss.at[slot], cot_rs.at[slot], delta, half)

    def each_cot(act):
        for delta in (-1, 1):
            @pl.when(there(delta))
            def _(delta=delta):
                act(cot_copy(delta))

    ro_copy = send(ro.at[half], ro.at[half], ro_ss.at[0], ro_rs.at[0], 0, mate)

    ro_copy.start()
    each_cot(lambda c: c.start())
    each_emb(lambda c: c.start())
    for k, a in every_w:
        w_copy(k, a).start()
    n_i = lax.broadcasted_iota(jnp.int32, (64, 128), 0)
    d_i = lax.broadcasted_iota(jnp.int32, (64, 128), 1)
    order = jnp.where(d_i == Q * (n_i % 16) + n_i // 16, 1.0, 0.0).astype(BF16)

    send(ro.at[half], ro.at[mate], ro_ss.at[0], ro_rs.at[0], 0, mate).wait_recv()
    for delta in (-1, 1):
        @pl.when(there(delta))
        def _(delta=delta):
            slot = (1 + delta) // 2
            send(
                cot.at[pl.ds(16, 16)], cot.at[pl.ds(16 + 16 * delta, 16)],
                cot_ss.at[slot], cot_rs.at[slot], delta, half,
            ).wait_recv()
    readout = jnp.concatenate([ro[0, 0:1], ro[1, 0:1]], axis=1)
    parts = split3(readout)
    row_i = lax.broadcasted_iota(jnp.int32, (16, 256), 0)
    ro_rows = sum(
        jnp.where(row_i == m, jnp.broadcast_to(part.astype(F32), (16, 256)), 0.0) for m, part in enumerate(parts)
    ).astype(BF16)
    cot_win = jnp.concatenate([cot[pl.ds(16 + bin_of(v), 1), :] for v in range(16)], axis=0)
    cot_t = sum(nt(order, part) for part in split3(cot_win))

    for v in range(16):
        columns[v] = jnp.broadcast_to(cot_t[:, v : v + 1], (64, 128))

    def emb_wait(k, chan):
        send(block, emb.at[k, chan], emb_ss.at[k, chan], emb_rs.at[k, chan], 0, mate).wait_recv()

    for k in range(BACK + AHEAD + 1):
        if k == BACK:
            emb_wait(k, mate)
        else:
            @pl.when(there(k - BACK))
            def _(k=k):
                for chan in range(2):
                    emb_wait(k, chan)

    for k in range(BACK + AHEAD + 1):
        for c in range(2):
            rwin[c, 16 * k : 16 * k + 16] = emb[k, c, 0:16].astype(F32)
            if k < 3:
                rwin[2 + c, 16 * k : 16 * k + 16] = emb[k, c, 16:32].astype(F32)

    outer_edge = jnp.logical_or(
        jnp.logical_and(half == 0, slab == 0), jnp.logical_and(half == 1, slab == slabs - 1)
    )

    def clear(buf, r):
        @pl.when(outer_edge)
        def _():
            buf[r + 8 :] = jnp.zeros((buf.shape[0] - r - 8,) + buf.shape[1:], BF16)

    def rim(n, buf, r):
        return [
            send(buf.at[r + j], buf.at[r - 1 - j], rim_ss.at[n, j], rim_rs.at[n, j], 0, mate)
            for j in range(r)
        ]

    rims = [rim(n, buf, r) for n, (buf, r) in enumerate([(p1, 2), (p2, 4), (d2, 4), (d1, 2), (d0, 1)])]

    def rim_start(n):
        for copy in rims[n]:
            copy.start()

    def rim_wait(n):
        for copy in rims[n]:
            copy.wait_recv()

    def first_pair(row, unused):
        place = 16 + bin_of(row - 1)
        left = jnp.concatenate([rwin[2 + c, pl.ds(place, 1), :] for c in range(2)], axis=1)
        tiles = [
            left + jnp.concatenate([rwin[c, pl.ds(place + q, 16, stride=Q), :] for c in range(2)], axis=1)
            for q in range(Q)
        ]
        put(p0, row, jnp.stack(tiles)[None], 1)
        return unused

    lax.fori_loop(0, 24, first_pair, 0)
    clear(p0, 1)

    taps = [2 - 2 * half, 1, 2 * half]

    def weights(k):
        local[k].wait()
        for a in range(3):
            send(w_hbm.at[k, a], w.at[mate, k, a], w_ss.at[k, a], w_rs.at[k, a], 0, mate).wait_recv()

    def forward(k, src, steps, n, sink):
        r = 2**k
        weights(k)

        def step(index, unused):
            begin = index * n
            wide = jnp.concatenate(
                [jnp.concatenate([w[c, k, a].reshape(3 * 256, 128) for a in taps], axis=0) for c in range(2)],
                axis=1,
            )
            lhs = jnp.concatenate(
                [
                    src[pl.ds(begin + m * r, n), b * r : b * r + Q].reshape(n * 64, 256)
                    for m in range(3) for b in range(3)
                ],
                axis=1,
            )
            z = sum(
                jnp.dot(lhs[:, m : m + 768], wide[m : m + 768], preferred_element_type=F32) for m in (0, 768, 1536)
            ).reshape(n, Q, 16, 256)
            s = 0.5 + 0.5 * jnp.tanh(0.5 * z)
            old = src[pl.ds(begin + r, n), r : r + Q].astype(F32)
            zs = z * s
            sink(index, begin, n, old + zs, s + zs * (1.0 - s))
            return unused

        lax.fori_loop(0, steps, step, 0)

    def rim_after(index, n_rim):
        @pl.when(index == 0)
        def _():
            rim_start(n_rim)

    def keep(buf, r, slopes, n_rim):
        def sink(index, begin, n, x, slope):
            put(buf, begin + r, x, r)
            rim_after(index, n_rim)
            slopes[pl.ds(begin, n)] = slope

        return sink

    forward(0, p0, 2, 11, keep(p1, 2, s0, 0))
    clear(p1, 2)
    each_emb(lambda c: c.wait_send())
    ro_copy.wait_send()
    each_cot(lambda c: c.wait_send())
    rim_wait(0)
    forward(1, p1, 2, 10, keep(p2, 4, s1, 1))
    clear(p2, 4)

    def last_sink(index, begin, n, x, slope):
        column = columns[pl.ds(begin, n)]
        grad = jnp.concatenate([column, column], axis=2) * readout[None]
        grad = grad.reshape(n, Q, 16, 256)
        put(d2, begin + 4, grad * slope, 4)
        rim_after(index, 2)
        g2[pl.ds(begin, n)] = grad
        p3[pl.ds(begin, n)] = x.astype(BF16)

    rim_wait(1)
    forward(2, p2, 2, 8, last_sink)
    clear(d2, 4)
    def backward(k, src, steps, n, before, sink):
        r = 2**k

        def step(index, unused):
            begin = index * n
            wide = jnp.concatenate([w[c, k, a, b] for a in taps for b in range(3) for c in range(2)], axis=1)
            lhs = jnp.concatenate(
                [
                    src[pl.ds(begin + (2 - m) * r, n), (2 - b) * r : (2 - b) * r + Q].reshape(n * 64, 256)
                    for m in range(3) for b in range(3)
                ],
                axis=1,
            )
            sink(index, begin, n, before[pl.ds(begin, n)] + sum(
                nt(lhs[:, m : m + 768], wide[:, m : m + 768]) for m in (0, 768, 1536)
            ).reshape(n, Q, 16, 256))
            return unused

        lax.fori_loop(0, steps, step, 0)

    def hand_on(buf, r, slopes, grads, n_rim):
        def sink(index, begin, n, grad):
            put(buf, begin + r, grad * slopes[pl.ds(begin, n)], r)
            rim_after(index, n_rim)
            grads[pl.ds(begin, n)] = grad

        return sink

    def last(index, begin, n, grad):
        g0[pl.ds(begin, n)] = grad

    rim_wait(2)
    backward(2, d2, 2, 6, g2, hand_on(d1, 2, s1, g1, 3))
    clear(d1, 2)
    rim_wait(3)
    backward(1, d1, 2, 5, g1, hand_on(d0, 1, s0, g0, 4))
    clear(d0, 1)
    rim_wait(4)
    backward(0, d0, 1, 8, g0, last)

    def v_of(u):
        return (1 - half) * (7 - u) + half * u

    spread[...] = jnp.zeros(spread.shape, F32)
    for t in range(8 + Q - 1):
        total = sum(g0[v_of(t - q), q] for q in range(Q) if 0 <= t - q < 8)
        place = pl.ds(8 + t, 16, stride=Q)
        for c in range(2):
            spread[c, place, :] = spread[c, place, :] + total[:, 128 * c : 128 * c + 128]

    def rg_source(k, chan):
        return spread.at[chan, pl.ds(pl.multiple_of(8 - 8 * half + 16 * k, 8), 16)]

    def rg_copy(k, chan):
        return send(rg_source(k, chan), rg.at[k, half], rg_ss.at[k, chan], rg_rs.at[k, half], k, chan)

    def each_rg(act):
        for k in (4, 3, 2, 1, 0):
            if k == 0:
                act(rg_copy(0, mate))
            else:
                @pl.when(there(k))
                def _(k=k):
                    for chan in range(2):
                        act(rg_copy(k, chan))

    each_rg(lambda c: c.start())
    contacts = [
        jnp.sum(nt(ro_rows, p3[v].reshape(64, 256)), axis=0, keepdims=True) for v in range(8)
    ]
    outwards = jnp.concatenate(contacts, axis=0)
    inwards = jnp.concatenate(contacts[::-1], axis=0)
    contact_rows = jnp.where(half == 1, outwards, inwards)
    contact = sum(jnp.dot(part, order, preferred_element_type=F32) for part in split3(contact_rows))

    lg = jnp.concatenate(
        [jnp.sum(g0[v_of(u)].reshape(64, 256), axis=0, keepdims=True) for u in range(8)], axis=0
    )
    low, high = lg[:, :128], lg[:, 128:]
    swap_out[0:8] = jnp.where(half == 0, high, low)
    swap_out[8:16] = contact
    swap_copy = send(swap_out, swap, swap_ss.at[0], swap_rs.at[0], 0, mate)
    swap_copy.start()
    rg[0, half] = spread[half, pl.ds(pl.multiple_of(8 - 8 * half, 8), 16), :]
    mine = pl.ds(pl.multiple_of(8 * half, 8), 8)
    other = pl.ds(pl.multiple_of(8 * mate, 8), 8)
    lg_out[mine, :] = jnp.where(half == 0, low, high)
    contact_out[mine, :] = contact[:, :64]

    for k in range(1, 5):
        @pl.when(jnp.logical_not(there(-k)))
        def _(k=k):
            rg[k] = jnp.zeros(rg.shape[1:], F32)

    for k, a in every_w:
        w_copy(k, a).wait_send()
    for copies in rims:
        for copy in copies:
            copy.wait_send()
    each_rg(lambda c: c.wait_send())
    swap_copy.wait_send()
    swap_copy.wait_recv()
    lg_out[other, :] = swap[0:8]
    contact_out[other, :] = swap[8:16, :64]

    def rg_wait(k, chan):
        send(rg_source(k, chan), rg.at[k, chan], rg_ss.at[k, chan], rg_rs.at[k, chan], 0, mate).wait_recv()

    for k in range(5):
        if k == 0:
            rg_wait(0, mate)
        else:
            @pl.when(there(-k))
            def _(k=k):
                for chan in range(2):
                    rg_wait(k, chan)
    rg_out[...] = sum(rg[k, c] for k in range(5) for c in range(2))


def hand_out(*refs):
    sems = refs[6]
    copies = [pltpu.make_async_copy(refs[n], refs[3 + n], sems.at[n]) for n in range(3)]
    for copy in copies:
        copy.start()
    for copy in copies:
        copy.wait()


def local(slabs, left_embed, right_embed, conv_weight, readout, cotangent):
    vmem = pl.BlockSpec(memory_space=pltpu.VMEM)
    anywhere = pl.BlockSpec(memory_space=pl.ANY)
    dma = pltpu.SemaphoreType.DMA

    def padded(rows, r):
        return pltpu.VMEM((rows, Q + 2 * r, 16, 256), BF16)

    def wide(rows):
        return pltpu.VMEM((rows, Q, 16, 256), F32)

    out_shape = (
        jax.ShapeDtypeStruct((16, 64), F32),
        jax.ShapeDtypeStruct((16, 128), F32),
        jax.ShapeDtypeStruct((16, 128), F32),
    )
    results = pl.pallas_call(
        functools.partial(kernel, slabs),
        out_shape=out_shape,
        in_specs=[vmem, vmem, anywhere, vmem, vmem],
        out_specs=(vmem, vmem, vmem),
        scratch_shapes=[
            pltpu.VMEM((32, 128), BF16),
            pltpu.VMEM((7, 2, 32, 128), BF16),
            pltpu.VMEM((4, 112, 128), F32),
            pltpu.VMEM((2, 3, 3, 3, 256, 128), BF16),
            pltpu.VMEM((48, 128), F32),
            pltpu.VMEM((2, 8, 128), F32),
            padded(24, 1), padded(24, 2), padded(24, 4),
            padded(20, 4), padded(14, 2), padded(11, 1),
            wide(22), wide(20), wide(16), wide(12), wide(10),
            pltpu.VMEM((16, 64, 128), F32), pltpu.VMEM((16, Q, 16, 256), BF16),
            pltpu.VMEM((2, 88, 128), F32),
            pltpu.VMEM((5, 2, 16, 128), F32),
            pltpu.VMEM((16, 128), F32),
            pltpu.VMEM((16, 128), F32),
            dma((7, 2)), dma((7, 2)), dma((3,)), dma((3, 3)), dma((3, 3)),
            dma((2,)), dma((2,)), dma((1,)), dma((1,)),
            dma((5, 2)), dma((5, 2)), dma((1,)), dma((1,)),
            dma((5, 4)), dma((5, 4)),
        ],
        compiler_params=pltpu.CompilerParams(
            collective_id=0, has_side_effects=True, vmem_limit_bytes=56 * 2**20
        ),
        cost_estimate=pl.CostEstimate(flops=8 * 10**9, bytes_accessed=4 * 10**6, transcendentals=10**6),
    )(left_embed, right_embed, conv_weight, readout.reshape(1, 128), cotangent)
    return pl.pallas_call(
        hand_out, out_shape=out_shape, in_specs=[anywhere] * 3, out_specs=(anywhere,) * 3,
        scratch_shapes=[dma((3,))],
    )(*results)


def solution(mesh):
    return jax.shard_map(
        functools.partial(local, mesh.shape["chrom"]),
        mesh=mesh,
        in_specs=(
            P("chrom", "chan"),
            P("chrom", "chan"),
            P(None, None, None, None, "chan"),
            P("chan"),
            P("chrom", None),
        ),
        out_specs=(P("chrom", None), P("chrom", "chan"), P("chrom", "chan")),
        check_vma=False,
    )
```
